256 devices in a mesh: dp: 4 (over y), rows: 64 (over x, z, core).
Axes of the slice: x: 4, y: 4, z: 8, core: 2. Of those that a mesh axis runs over, the one named last changes fastest.
Arguments:
- grad: bfloat16 [4, 4096, 12288], P('dp', 'rows'), may hold values from -60 to 60
- error: bfloat16 [4, 4096, 12288], P('dp', 'rows'), may hold values from -3 to 3
- momentum: float32 [4096, 12288], P('rows'), may hold values from -3 to 3
- q_start: float32 [12288, 16], replicated, may hold values from -5 to 5
Outputs:
- new_error: bfloat16 [4, 4096, 12288], P('dp', 'rows')
- new_momentum: float32 [4096, 12288], P('rows')
- q_next: float32 [12288, 16], replicated
The draws below stay inside these ranges and needn't reach their ends.
All inputs are finite; a program needn't handle non-finite values.
Results may differ from the reference program's by a relative error of at most 0.006.
Values sent between devices are 32-bit elements; how exact they have to be, the bound alone decides.
No kernel may reach another device: no remote copies, remote signals or barrier semaphores. Data moves between devices by JAX's collectives and lax.ppermute only.
A program may use at most 64 MiB of HBM per device.

```python
import math
import jax
import jax.numpy as jnp
from jax import lax

ROWS = 4096
COLS = 12288
RANK = 16
GROUPS = 4


def draw_grad(key, part):
    key = jax.random.fold_in(key, 11)
    first, second, third = jax.random.split(key, 3)
    row_scale = jnp.exp(jax.random.uniform(second, (GROUPS, ROWS, 1), jnp.float32) * math.log(10.0))
    col_scale = jnp.exp(jax.random.uniform(third, (1, 1, COLS), jnp.float32) * math.log(3.0))
    base = jnp.clip(jax.random.normal(first, (GROUPS, ROWS, COLS), jnp.float32), -6.0, 6.0)
    values = 0.3 * base * row_scale * col_scale
    return values.astype(jnp.bfloat16)


def block_scale(rng, dims, cuts, smallest, largest):
    level = 1.0
    for position, shards_of in cuts:
        steps = jax.random.uniform(jax.random.fold_in(jax.random.fold_in(rng, 6), position), (shards_of,), jnp.float32, smallest / len(cuts), largest / len(cuts))
        level = level * jnp.repeat(jnp.exp(steps), dims[position] // shards_of).reshape((-1,) + (1,) * (len(dims) - 1 - position))
    return level


def noise(rng, extent, spread, bound, cuts=(), kind=jnp.bfloat16):
    drawn = spread * jax.random.normal(rng, extent, jnp.float32)
    if cuts:
        drawn = drawn * block_scale(rng, extent, cuts, -0.22, 0.18)
    return jnp.clip(drawn, -bound, bound).astype(kind)


def setup_inputs(seed: int = 0) -> dict:
    streams_of = jax.random.split(jax.random.key(seed), 5)
    grad = draw_grad(jax.random.fold_in(streams_of[4], 71), 0)
    error = noise(streams_of[1], (GROUPS, ROWS, COLS), 0.5, 3.0, ((0, 4), (1, 64)))
    momentum = noise(streams_of[2], (ROWS, COLS), 0.5, 3.0, ((0, 64),), jnp.float32)
    q_start = noise(streams_of[3], (COLS, RANK), 1.0, 5.0, (), jnp.float32)
    return {"grad": grad, "error": error, "momentum": momentum, "q_start": q_start}


def reference(grad, error, momentum, q_start):
    q_low = q_start.astype(jnp.bfloat16)

    def merged_of(index):
        summed = grad[index].astype(jnp.float32) + error[index].astype(jnp.float32)
        return (summed, summed.astype(jnp.bfloat16))

    def left_step(total, index):
        summed, merged = merged_of(index)
        return (total + jnp.dot(merged.astype(jnp.float32), q_low.astype(jnp.float32), preferred_element_type=jnp.float32), None)
    left, unused = lax.scan(left_step, jnp.zeros((ROWS, RANK), jnp.float32), jnp.arange(GROUPS, dtype=jnp.int32))
    gram = jnp.dot(left.T, left, precision=lax.Precision.HIGHEST)
    lower = jnp.linalg.cholesky(gram)
    ortho = jax.scipy.linalg.solve_triangular(lower, left.T, lower=True).T
    left_low = left.astype(jnp.bfloat16)

    def right_step(total, index):
        summed, merged = merged_of(index)
        term = lax.dot_general(merged.astype(jnp.float32), left_low.astype(jnp.float32), (((0,), (0,)), ((), ())), preferred_element_type=jnp.float32)
        return (total + term, None)
    right, unused = lax.scan(right_step, jnp.zeros((COLS, RANK), jnp.float32), jnp.arange(GROUPS, dtype=jnp.int32))
    q_next = jax.scipy.linalg.solve_triangular(lower, right.T, lower=True).T / GROUPS
    approx = jnp.dot(ortho, q_next.T, precision=lax.Precision.HIGHEST)

    def error_of(index):
        summed, merged = merged_of(index)
        return (summed - approx).astype(jnp.bfloat16)
    new_error = lax.map(error_of, jnp.arange(GROUPS, dtype=jnp.int32))
    new_momentum = 0.9 * momentum + approx
    return (new_error, new_momentum, q_next)
```

```python
import jax
import jax.numpy as jnp
from jax import lax
from jax.sharding import Mesh, PartitionSpec as P

HIGHEST = lax.Precision.HIGHEST


def split3(value):
    high = lax.reduce_precision(value, 8, 7)
    rest = value - high
    middle = lax.reduce_precision(rest, 8, 7)
    low = rest - middle
    return tuple(part.astype(jnp.bfloat16) for part in (high, middle, low))


def packed_dot(first, second):
    a, b, c = split3(first)
    d, e, f = split3(second)
    return jnp.dot(
        jnp.concatenate([a, a, b, a, b, c], axis=1),
        jnp.concatenate([d, e, d, f, e, d], axis=0),
        preferred_element_type=jnp.float32,
    )


def shards(grad, error, momentum, q_start):
    groups = lax.axis_size("dp")
    planes = groups * lax.axis_size("x")
    layers = lax.axis_size("z")
    rank = q_start.shape[1]
    cols = grad.shape[-1]
    half = cols // 2
    piece = half // planes
    core = lax.axis_index("core")

    summed = grad[0].astype(jnp.float32) + error[0].astype(jnp.float32)
    merged = summed.astype(jnp.bfloat16)
    q_low = q_start.T.astype(jnp.bfloat16)
    term = lax.dot_general(q_low, merged, (((1,), (1,)), ((), ())), preferred_element_type=jnp.float32)
    one, two, three = (
        lax.ppermute(term, "dp", [(i, (i + k) % groups) for i in range(groups)]) for k in (1, 2, 3)
    )
    left = (term + two) + (one + three)

    right = jnp.dot(left.astype(jnp.bfloat16), merged, preferred_element_type=jnp.float32)
    gram = lax.dot_general(left, left, (((1,), (1,)), ((), ())), precision=HIGHEST)
    gram = jnp.pad(gram, ((0, 0), (0, 128 - rank)))

    kept = lax.dynamic_slice_in_dim(right, core * half, half, 1)
    given = lax.dynamic_slice_in_dim(right, (1 - core) * half, half, 1)
    swap = [(0, 1), (1, 0)]
    kept = kept + lax.ppermute(given, "core", swap)
    gram = gram + lax.ppermute(gram, "core", swap)

    pieces = kept.reshape(rank, planes, piece).transpose(1, 0, 2)
    pieces = jnp.concatenate([pieces, jnp.broadcast_to(gram[None], (planes,) + gram.shape)], axis=2)
    part = lax.all_to_all(pieces, ("dp", "x"), 0, 0).sum(0)
    part = lax.all_to_all(jnp.broadcast_to(part[None], (layers,) + part.shape), "z", 0, 0).sum(0)
    gram = part[:, piece : piece + rank] / groups
    part = part[:, :piece]
    own = lax.all_to_all(jnp.broadcast_to(part[None], (planes,) + part.shape), ("dp", "x"), 0, 0)
    own = own.transpose(1, 0, 2).reshape(rank, half)
    other = lax.ppermute(own, "core", swap)
    right = jnp.concatenate([jnp.where(core == 0, own, other), jnp.where(core == 0, other, own)], axis=1)

    lower = jnp.linalg.cholesky(gram)
    inverse = jax.scipy.linalg.solve_triangular(lower, jnp.eye(rank, dtype=jnp.float32), lower=True)
    ortho = jnp.dot(inverse, left, precision=HIGHEST).T
    q_next = packed_dot(inverse, right) / groups
    approx = packed_dot(ortho, q_next)
    new_error = (summed - approx).astype(jnp.bfloat16)[None]
    new_momentum = 0.9 * momentum + approx
    return (new_error, new_momentum, q_next.T)


def solution(mesh):
    shape = mesh.shape
    fine = Mesh(mesh.devices.reshape(shape["dp"], 4, 8, 2), ("dp", "x", "z", "core"))
    rows = ("x", "z", "core")
    placed = (P("dp", rows, None), P("dp", rows, None), P(rows, None), P())
    return jax.shard_map(
        shards,
        mesh=fine,
        in_specs=placed,
        out_specs=(P("dp", rows, None), P(rows, None), P()),
        check_vma=False,
    )
```

```python
import functools
import jax
import jax.numpy as jnp
from jax import lax
from jax.experimental import pallas as pl
from jax.experimental.pallas import tpu as pltpu
from jax.sharding import Mesh, PartitionSpec as P

HIGHEST = lax.Precision.HIGHEST
F32 = jnp.float32
BF16 = jnp.bfloat16
LANES = 128
WHOLE = pl.BlockSpec(memory_space=pltpu.VMEM)
SCALAR = pl.BlockSpec(memory_space=pltpu.SMEM)
FAR = pl.BlockSpec(memory_space=pltpu.HBM)


def split3(value):
    high = value.astype(BF16)
    rest = value - high.astype(F32)
    middle = rest.astype(BF16)
    low = (rest - middle.astype(F32)).astype(BF16)
    return high, middle, low


def nt_dot(first, second, precision=None):
    return lax.dot_general(
        first, second, (((1,), (1,)), ((), ())), precision=precision, preferred_element_type=F32
    )


def left_kernel(chunk, grad, error, q_start, term, merged, base, grad_vmem, error_vmem, q_vmem, sems):
    count = grad.shape[1] // chunk
    copies = []
    for step in range(count):
        here = pl.ds(step * chunk, chunk)
        group = [
            pltpu.make_async_copy(far.at[:, here], near.at[:, here], sems.at[which, step])
            for which, (far, near) in enumerate(
                ((grad, grad_vmem), (error, error_vmem), (q_start, q_vmem))
            )
        ]
        for copy in group:
            copy.start()
        copies.append(group)
    total = jnp.zeros(term.shape, F32)
    for step in range(count):
        for copy in copies[step]:
            copy.wait()
        here = pl.ds(step * chunk, chunk)
        summed = grad_vmem[:, here].astype(F32) + error_vmem[:, here].astype(F32)
        base[:, here] = summed
        low = summed.astype(BF16)
        merged[:, here] = low
        total += nt_dot(q_vmem[:, here].astype(BF16), low)
    term[...] = total


def given_kernel(core, term, one, two, three, merged, given, left):
    half = merged.shape[1] // 2
    rank = term.shape[0]
    total = (term[...] + two[...]) + (one[...] + three[...])
    left[...] = total
    there = pl.ds(pl.multiple_of((1 - core[0]) * half, LANES), half)
    given[:, :half] = jnp.dot(total.astype(BF16), merged[:, there], preferred_element_type=F32)
    given[:, half:] = jnp.zeros((rank, LANES), F32)
    given[:, half : half + rank] = nt_dot(total, total, HIGHEST)


def kept_kernel(core, left, merged, kept):
    half = merged.shape[1] // 2
    here = pl.ds(pl.multiple_of(core[0] * half, LANES), half)
    kept[...] = jnp.dot(left[...].astype(BF16), merged[:, here], preferred_element_type=F32)


def pieces_kernel(kept, given, taken, pieces):
    half = kept.shape[1]
    planes = pieces.shape[0]
    piece = half // planes
    gram = given[:, half:] + taken[:, half:]
    for index in range(planes):
        here = pl.ds(index * piece, piece)
        pieces[index, :, :piece] = kept[:, here] + taken[:, here]
        pieces[index, :, piece:] = gram


def plane_kernel(arrived, spread):
    total = arrived[0]
    for index in range(1, arrived.shape[0]):
        total += arrived[index]
    for index in range(spread.shape[0]):
        spread[index] = total


def layer_kernel(groups, arrived, spread, gram):
    piece = spread.shape[2]
    total = arrived[0]
    for index in range(1, arrived.shape[0]):
        total += arrived[index]
    gram[...] = total[:, piece:] / groups
    for index in range(spread.shape[0]):
        spread[index] = total[:, :piece]


def factor_kernel(groups, gram, left, factors):
    rank, rows = left.shape
    row = lax.broadcasted_iota(jnp.int32, gram.shape, 0)
    col = lax.broadcasted_iota(jnp.int32, gram.shape, 1)
    table = jnp.where(col == row + rank, 1.0, gram[...])
    for step in range(rank):
        scaled = table[step : step + 1, :] / jnp.sqrt(table[step : step + 1, step : step + 1])
        coef = table[:, step : step + 1] / jnp.sqrt(table[step : step + 1, step : step + 1])
        table = jnp.where(row > step, table - coef * scaled, jnp.where(row == step, scaled, table))
    inverse = table[:, rank : 2 * rank]
    ortho = jnp.dot(inverse, left[...], precision=HIGHEST, preferred_element_type=F32)
    combined = lax.dot_general(
        ortho, inverse, (((0,), (0,)), ((), ())), precision=HIGHEST, preferred_element_type=F32
    )
    stacked = jnp.concatenate([combined, inverse], axis=0) / groups
    high, middle, low = split3(stacked)
    factors[...] = jnp.concatenate([high, high, middle, high, middle, low], axis=1)


def final_kernel(core, factors, own, other, base, momentum, new_error, new_momentum, q_next):
    step = pl.program_id(0)
    steps = pl.num_programs(0)
    cols = new_error.shape[1]
    piece = own.shape[2]
    rows = new_error.shape[0]
    per = cols // piece
    mine = step < steps // 2
    inner = lax.rem(step, steps // 2)
    block = jnp.where(mine, core[0], 1 - core[0]) * (steps // 2) + inner

    def run(source):
        for index in range(per):
            high, middle, low = split3(source[inner * per + index])
            depth = jnp.concatenate([high, middle, high, low, middle, high], axis=0)
            product = jnp.dot(factors[...], depth, preferred_element_type=F32)
            approx = product[:rows]
            here = pl.ds(index * piece, piece)
            there = pl.ds(pl.multiple_of(block * cols + index * piece, LANES), piece)
            q_next[:, here] = product[rows:]
            new_error[:, here] = (base[:, there] - approx).astype(BF16)
            new_momentum[:, here] = 0.9 * momentum[:, there] + approx

    @pl.when(mine)
    def _():
        run(own)

    @pl.when(jnp.logical_not(mine))
    def _():
        run(other)


def params(megabytes):
    return pltpu.CompilerParams(vmem_limit_bytes=megabytes * 1024 * 1024)


def cost(flops, moved):
    return pl.CostEstimate(flops=flops, bytes_accessed=moved, transcendentals=0)


def shards(grad, error, momentum, q_start):
    groups = lax.axis_size("dp")
    planes = groups * lax.axis_size("x")
    layers = lax.axis_size("z")
    cols, rank = q_start.shape
    rows = grad.shape[1]
    half = cols // 2
    piece = half // planes
    core = lax.axis_index("core").astype(jnp.int32).reshape(1)
    swap = [(0, 1), (1, 0)]
    chunk = cols // 6

    term, merged, base = pl.pallas_call(
        functools.partial(left_kernel, chunk),
        out_shape=(
            pltpu.VMEM((rank, rows), F32),
            pltpu.VMEM((rows, cols), BF16),
            pltpu.VMEM((rows, cols), F32),
        ),
        in_specs=[FAR] * 3,
        out_specs=(WHOLE,) * 3,
        scratch_shapes=[
            pltpu.VMEM((rows, cols), BF16),
            pltpu.VMEM((rows, cols), BF16),
            pltpu.VMEM((rank, cols), F32),
            pltpu.SemaphoreType.DMA((3, cols // chunk)),
        ],
        compiler_params=params(58),
        name="left_term",
    )(grad[0], error[0], q_start.T)
    one, two, three = (
        lax.ppermute(term, "dp", [(i, (i + k) % groups) for i in range(groups)]) for k in (1, 2, 3)
    )
    given, left = pl.pallas_call(
        given_kernel,
        out_shape=(pltpu.VMEM((rank, half + LANES), F32), pltpu.VMEM((rank, rows), F32)),
        in_specs=[SCALAR] + [WHOLE] * 5,
        out_specs=(WHOLE,) * 2,
        compiler_params=params(8),
        name="right_given",
    )(core, term, one, two, three, merged)
    taken = lax.ppermute(given, "core", swap)
    kept = pl.pallas_call(
        kept_kernel,
        out_shape=pltpu.VMEM((rank, half), F32),
        in_specs=[SCALAR] + [WHOLE] * 2,
        out_specs=WHOLE,
        compiler_params=params(8),
        cost_estimate=cost(2 * rank * rows * half, 4 * rows * half),
        name="right_kept",
    )(core, left, merged)
    pieces = pl.pallas_call(
        pieces_kernel,
        out_shape=pltpu.VMEM((planes, rank, piece + LANES), F32),
        in_specs=[WHOLE] * 3,
        out_specs=WHOLE,
        compiler_params=params(8),
        name="right_pieces",
    )(kept, given, taken)
    arrived = lax.all_to_all(pieces, ("dp", "x"), 0, 0)
    spread = pl.pallas_call(
        plane_kernel,
        out_shape=pltpu.VMEM((layers, rank, piece + LANES), F32),
        in_specs=[WHOLE],
        out_specs=WHOLE,
        compiler_params=params(8),
        name="plane_sum",
    )(arrived)
    arrived = lax.all_to_all(spread, "z", 0, 0)
    spread, gram = pl.pallas_call(
        functools.partial(layer_kernel, groups),
        out_shape=(pltpu.VMEM((planes, rank, piece), F32), pltpu.VMEM((rank, LANES), F32)),
        in_specs=[WHOLE],
        out_specs=(WHOLE,) * 2,
        compiler_params=params(8),
        name="layer_sum",
    )(arrived)
    own = lax.all_to_all(spread, ("dp", "x"), 0, 0)
    factors = pl.pallas_call(
        functools.partial(factor_kernel, groups),
        out_shape=pltpu.VMEM((rows + rank, 6 * rank), BF16),
        in_specs=[WHOLE] * 2,
        out_specs=WHOLE,
        compiler_params=params(8),
        cost_estimate=cost(8 * rank * rows * LANES, 4 * rows * LANES),
        name="factors",
    )(gram, left)
    other = lax.ppermute(own, "core", swap)

    steps = 8
    width = cols // steps
    place = lambda step, core: jnp.where(
        step < steps // 2, core[0] * (steps // 2) + step, (1 - core[0]) * (steps // 2) + step - steps // 2
    )
    block = lambda height: pl.BlockSpec((height, width), lambda step, core: (0, place(step, core)))
    new_error, new_momentum, q_next = pl.pallas_call(
        final_kernel,
        out_shape=(
            jax.ShapeDtypeStruct((rows, cols), BF16),
            jax.ShapeDtypeStruct((rows, cols), F32),
            jax.ShapeDtypeStruct((rank, cols), F32),
        ),
        grid_spec=pltpu.PrefetchScalarGridSpec(
            num_scalar_prefetch=1,
            grid=(steps,),
            in_specs=[WHOLE] * 5,
            out_specs=(block(rows), block(rows), block(rank)),
        ),
        compiler_params=params(16),
        name="outputs",
    )(core, factors, own, other, base, momentum)
    return (new_error[None], new_momentum, q_next.T)


def solution(mesh):
    shape = mesh.shape
    fine = Mesh(mesh.devices.reshape(shape["dp"], 4, 8, 2), ("dp", "x", "z", "core"))
    rows = ("x", "z", "core")
    placed = (P("dp", rows, None), P("dp", rows, None), P(rows, None), P())
    return jax.shard_map(
        shards,
        mesh=fine,
        in_specs=placed,
        out_specs=(P("dp", rows, None), P(rows, None), P()),
        check_vma=False,
    )
```

```python
import functools
import jax
import jax.numpy as jnp
from jax import lax
from jax.experimental import pallas as pl
from jax.experimental.pallas import tpu as pltpu
from jax.sharding import Mesh, PartitionSpec as P

HIGHEST = lax.Precision.HIGHEST
F32 = jnp.float32
BF16 = jnp.bfloat16
LANES = 128
TILE = 8
WHOLE = pl.BlockSpec(memory_space=pltpu.VMEM)
FAR = pl.BlockSpec(memory_space=pltpu.HBM)


def split3(value):
    high = value.astype(BF16)
    rest = value - high.astype(F32)
    middle = rest.astype(BF16)
    low = (rest - middle.astype(F32)).astype(BF16)
    return high, middle, low


def nt_dot(first, second, precision=None):
    return lax.dot_general(
        first, second, (((1,), (1,)), ((), ())), precision=precision, preferred_element_type=F32
    )


def left_kernel(chunk, grad, error, q_start, term, merged, base, grad_vmem, error_vmem, q_vmem, sems):
    count = grad.shape[1] // chunk
    copies = []
    for step in range(count):
        here = pl.ds(step * chunk, chunk)
        group = [
            pltpu.make_async_copy(far.at[:, here], near.at[:, here], sems.at[which, step])
            for which, (far, near) in enumerate(
                ((grad, grad_vmem), (error, error_vmem), (q_start, q_vmem))
            )
        ]
        for copy in group:
            copy.start()
        copies.append(group)
    total = jnp.zeros(term.shape, F32)
    for step in range(count):
        for copy in copies[step]:
            copy.wait()
        here = pl.ds(step * chunk, chunk)
        summed = grad_vmem[:, here].astype(F32) + error_vmem[:, here].astype(F32)
        base[:, here] = summed
        low = summed.astype(BF16)
        merged[:, here] = low
        total += nt_dot(q_vmem[:, here].astype(BF16), low)
    term[...] = total


def given_kernel(term, one, two, three, merged, given, gram, left):
    half = merged.shape[1] // 2
    rank = term.shape[0]
    total = (term[...] + two[...]) + (one[...] + three[...])
    left[...] = total
    there = pl.ds(pl.multiple_of((1 - lax.axis_index("core")) * half, LANES), half)
    given[:, :half] = jnp.dot(total.astype(BF16), merged[:, there], preferred_element_type=F32)
    square = nt_dot(total, total, HIGHEST)
    rest = jnp.zeros((TILE, LANES - 2 * rank), F32)
    tile = jnp.concatenate([square[:TILE], square[TILE:], rest], axis=1)
    gram[...] = tile
    given[:TILE, half:] = tile
    given[TILE:, half:] = jnp.zeros((rank - TILE, LANES), F32)


def kept_kernel(left, merged, kept):
    half = merged.shape[1] // 2
    here = pl.ds(pl.multiple_of(lax.axis_index("core") * half, LANES), half)
    kept[...] = jnp.dot(left[...].astype(BF16), merged[:, here], preferred_element_type=F32)


def pieces_kernel(kept, gram, taken, pieces):
    half = kept.shape[1]
    planes, tiles = pieces.shape[:2]
    across = (tiles - 1) // 2
    square = gram[...] + taken[:TILE, half:]
    for index in range(planes):
        for block in range(across):
            here = pl.ds((index * across + block) * LANES, LANES)
            total = kept[:, here] + taken[:, here]
            pieces[index, block] = total[:TILE]
            pieces[index, across + block] = total[TILE:]
        pieces[index, tiles - 1] = square


def plane_kernel(arrived, spread):
    total = arrived[0]
    for index in range(1, arrived.shape[0]):
        total += arrived[index]
    for index in range(spread.shape[0]):
        spread[index] = total


def layer_kernel(groups, arrived, spread, gram):
    tiles = spread.shape[1]
    total = arrived[0]
    for index in range(1, arrived.shape[0]):
        total += arrived[index]
    gram[...] = total[tiles] / groups
    for index in range(spread.shape[0]):
        spread[index] = total[:tiles]


def factor_kernel(groups, gram, left, factors):
    rank, rows = left.shape
    shape = (rank, LANES)
    row = lax.broadcasted_iota(jnp.int32, shape, 0)
    col = lax.broadcasted_iota(jnp.int32, shape, 1)
    third = (col >= rank) & (col < 2 * rank)
    square = jnp.concatenate([gram[:, :rank], gram[:, rank : 2 * rank]], axis=0)
    rest = jnp.zeros((rank, LANES - rank - rows), F32)
    table = jnp.concatenate([square, left[...], rest], axis=1)
    table = jnp.concatenate(
        [table[:, :rank], jnp.zeros((rank, rank), F32), table[:, rank : LANES - rank]], axis=1
    )
    table = jnp.where(col == row + rank, 1.0, table)
    roots = jnp.ones((rank, 1), F32)
    for step in range(rank):
        pivot = table[step : step + 1, step : step + 1]
        scaled = table[step : step + 1, :] / pivot
        column = table[:, step : step + 1]
        mine = row[:, :1] == step
        roots = jnp.where(mine, jnp.sqrt(pivot), roots)
        change = jnp.where((row < step) & third, 0.0, column * scaled)
        table = jnp.where(row == step, scaled, table - change)
    table = jnp.where(third, table * roots, table)
    combined = table[:, 2 * rank : 2 * rank + rows].T
    stacked = jnp.concatenate([combined, table[:, rank : 2 * rank]], axis=0) / groups
    high, middle, low = split3(stacked)
    factors[...] = jnp.concatenate([high, high, middle, high, middle, low], axis=1)


def output_kernel(chunks, mine, factors, source, base, momentum, *rest):
    new_error, new_momentum, q_next, error_vmem, momentum_vmem, q_vmem, sems = rest[-7:]
    core = lax.axis_index("core")
    rows, cols = base.shape
    half = cols // 2
    tiles = source.shape[1]
    across = tiles // 2
    width = half // chunks
    per = width // (across * LANES)
    begin = (core if mine else 1 - core) * half
    copies = []
    for chunk in range(chunks):
        parts = []
        for index in range(chunk * per, (chunk + 1) * per):
            for block in range(across):
                parts.append(jnp.concatenate([source[index, block], source[index, across + block]], axis=0))
        high, middle, low = split3(jnp.concatenate(parts, axis=1))
        depth = jnp.concatenate([high, middle, high, low, middle, high], axis=0)
        product = jnp.dot(factors[...], depth, preferred_element_type=F32)
        approx = product[:rows]
        here = pl.ds(chunk * width, width)
        there = pl.ds(pl.multiple_of(begin + chunk * width, LANES), width)
        q_vmem[:, here] = product[rows:]
        error_vmem[:, here] = (base[:, there] - approx).astype(BF16)
        momentum_vmem[:, here] = 0.9 * momentum[:, there] + approx
        for which, (near, far) in enumerate(
            ((error_vmem, new_error), (momentum_vmem, new_momentum), (q_vmem, q_next))
        ):
            copy = pltpu.make_async_copy(near.at[:, here], far.at[:, there], sems.at[which, chunk])
            copy.start()
            copies.append(copy)
    for copy in copies:
        copy.wait()


def params(megabytes):
    return pltpu.CompilerParams(vmem_limit_bytes=megabytes * 1024 * 1024)


def cost(flops, moved):
    return pl.CostEstimate(flops=flops, bytes_accessed=moved, transcendentals=0)


def shards(grad, error, momentum, q_start):
    groups = lax.axis_size("dp")
    planes = groups * lax.axis_size("x")
    layers = lax.axis_size("z")
    cols, rank = q_start.shape
    rows = grad.shape[1]
    half = cols // 2
    tiles = rank * half // planes // (TILE * LANES)
    swap = [(0, 1), (1, 0)]
    chunk = cols // 6

    term, merged, base = pl.pallas_call(
        functools.partial(left_kernel, chunk),
        out_shape=(
            pltpu.VMEM((rank, rows), F32),
            pltpu.VMEM((rows, cols), BF16),
            pltpu.VMEM((rows, cols), F32),
        ),
        in_specs=[FAR] * 3,
        out_specs=(WHOLE,) * 3,
        scratch_shapes=[
            pltpu.VMEM((rows, cols), BF16),
            pltpu.VMEM((rows, cols), BF16),
            pltpu.VMEM((rank, cols), F32),
            pltpu.SemaphoreType.DMA((3, cols // chunk)),
        ],
        compiler_params=params(58),
        name="left_term",
    )(grad[0], error[0], q_start.T)
    two, three, one = (
        lax.ppermute(term, "dp", [(i, (i + k) % groups) for i in range(groups)]) for k in (1, 3, 2)
    )
    one, two = two, one
    given, gram, left = pl.pallas_call(
        given_kernel,
        out_shape=(
            pltpu.VMEM((rank, half + LANES), F32),
            pltpu.VMEM((TILE, LANES), F32),
            pltpu.VMEM((rank, rows), F32),
        ),
        in_specs=[WHOLE] * 5,
        out_specs=(WHOLE,) * 3,
        compiler_params=params(8),
        name="right_given",
    )(term, one, two, three, merged)
    taken = lax.ppermute(given, "core", swap)
    kept = pl.pallas_call(
        kept_kernel,
        out_shape=pltpu.VMEM((rank, half), F32),
        in_specs=[WHOLE] * 2,
        out_specs=WHOLE,
        compiler_params=params(8),
        cost_estimate=cost(2 * rank * rows * half, 4 * rows * half),
        name="right_kept",
    )(left, merged)
    pieces = pl.pallas_call(
        pieces_kernel,
        out_shape=pltpu.VMEM((planes, tiles + 1, TILE, LANES), F32),
        in_specs=[WHOLE] * 3,
        out_specs=WHOLE,
        compiler_params=params(8),
        name="right_pieces",
    )(kept, gram, taken)
    arrived = lax.all_to_all(pieces, ("dp", "x"), 0, 0)
    spread = pl.pallas_call(
        plane_kernel,
        out_shape=pltpu.VMEM((layers, tiles + 1, TILE, LANES), F32),
        in_specs=[WHOLE],
        out_specs=WHOLE,
        compiler_params=params(8),
        name="plane_sum",
    )(arrived)
    arrived = lax.all_to_all(spread, "z", 0, 0)
    spread, gram = pl.pallas_call(
        functools.partial(layer_kernel, groups),
        out_shape=(pltpu.VMEM((planes, tiles, TILE, LANES), F32), pltpu.VMEM((TILE, LANES), F32)),
        in_specs=[WHOLE],
        out_specs=(WHOLE,) * 2,
        compiler_params=params(8),
        name="layer_sum",
    )(arrived)
    own = lax.all_to_all(spread, ("dp", "x"), 0, 0)
    factors = pl.pallas_call(
        functools.partial(factor_kernel, groups),
        out_shape=pltpu.VMEM((rows + rank, 6 * rank), BF16),
        in_specs=[WHOLE] * 2,
        out_specs=WHOLE,
        compiler_params=params(8),
        cost_estimate=cost(8 * rank * rows * LANES, 4 * rows * LANES),
        name="factors",
    )(gram, left)
    own, factors = lax.optimization_barrier((own, factors))
    other = lax.ppermute(own, "core", swap)

    chunks = 4

    def outputs(mine, source, before):
        shapes = (((rows, cols), BF16), ((rows, cols), F32), ((rank, cols), F32))
        return pl.pallas_call(
            functools.partial(output_kernel, chunks, mine),
            out_shape=tuple(jax.ShapeDtypeStruct(shape, dtype) for shape, dtype in shapes),
            in_specs=[WHOLE] * 4 + [FAR] * len(before),
            out_specs=(FAR,) * 3,
            scratch_shapes=[pltpu.VMEM((shape[0], half), dtype) for shape, dtype in shapes]
            + [pltpu.SemaphoreType.DMA((3, chunks))],
            input_output_aliases={4 + index: index for index in range(len(before))},
            compiler_params=params(8),
            cost_estimate=cost(12 * rank * (rows + rank) * half, 18 * rows * half),
            name="outputs_own" if mine else "outputs_other",
        )(factors, source, base, momentum, *before)

    new_error, new_momentum, q_next = outputs(False, other, outputs(True, own, ()))
    return (new_error[None], new_momentum, q_next.T)


def solution(mesh):
    shape = mesh.shape
    fine = Mesh(mesh.devices.reshape(shape["dp"], 4, 8, 2), ("dp", "x", "z", "core"))
    rows = ("x", "z", "core")
    placed = (P("dp", rows, None), P("dp", rows, None), P(rows, None), P())
    return jax.shard_map(
        shards,
        mesh=fine,
        in_specs=placed,
        out_specs=(P("dp", rows, None), P(rows, None), P()),
        check_vma=False,
    )
```

```python
import functools
import jax
import jax.numpy as jnp
from jax import lax
from jax.experimental import pallas as pl
from jax.experimental.pallas import tpu as pltpu
from jax.sharding import Mesh, PartitionSpec as P

HIGHEST = lax.Precision.HIGHEST
F32 = jnp.float32
BF16 = jnp.bfloat16
LANES = 128
TILE = 8
WHOLE = pl.BlockSpec(memory_space=pltpu.VMEM)
FAR = pl.BlockSpec(memory_space=pltpu.HBM)


def split3(value):
    high = value.astype(BF16)
    rest = value - high.astype(F32)
    middle = rest.astype(BF16)
    low = (rest - middle.astype(F32)).astype(BF16)
    return high, middle, low


def nt_dot(first, second, precision=None):
    return lax.dot_general(
        first, second, (((1,), (1,)), ((), ())), precision=precision, preferred_element_type=F32
    )


def left_kernel(chunk, grad, error, q_start, term, merged, base, grad_vmem, error_vmem, q_vmem, sems):
    count = grad.shape[1] // chunk
    copies = []
    for step in range(count):
        here = pl.ds(step * chunk, chunk)
        group = [
            pltpu.make_async_copy(far.at[:, here], near.at[:, here], sems.at[which, step])
            for which, (far, near) in enumerate(
                ((grad, grad_vmem), (error, error_vmem), (q_start, q_vmem))
            )
        ]
        for copy in group:
            copy.start()
        copies.append(group)
    total = jnp.zeros(term.shape, F32)
    for step in range(count):
        for copy in copies[step]:
            copy.wait()
        here = pl.ds(step * chunk, chunk)
        summed = grad_vmem[:, here].astype(F32) + error_vmem[:, here].astype(F32)
        base[:, here] = summed
        low = summed.astype(BF16)
        merged[:, here] = low
        total += nt_dot(q_vmem[:, here].astype(BF16), low)
    term[...] = total


def given_kernel(term, one, two, three, merged, given, gram, left):
    half = merged.shape[1] // 2
    rank = term.shape[0]
    total = (term[...] + two[...]) + (one[...] + three[...])
    left[...] = total
    there = pl.ds(pl.multiple_of((1 - lax.axis_index("core")) * half, LANES), half)
    given[:, :half] = jnp.dot(total.astype(BF16), merged[:, there], preferred_element_type=F32)
    square = nt_dot(total, total, HIGHEST)
    rest = jnp.zeros((TILE, LANES - 2 * rank), F32)
    tile = jnp.concatenate([square[:TILE], square[TILE:], rest], axis=1)
    gram[...] = tile
    given[:TILE, half:] = tile
    given[TILE:, half:] = jnp.zeros((rank - TILE, LANES), F32)


def kept_kernel(left, merged, kept):
    half = merged.shape[1] // 2
    here = pl.ds(pl.multiple_of(lax.axis_index("core") * half, LANES), half)
    kept[...] = jnp.dot(left[...].astype(BF16), merged[:, here], preferred_element_type=F32)


def pieces_kernel(kept, gram, taken, pieces):
    half = kept.shape[1]
    planes, tiles = pieces.shape[:2]
    across = (tiles - 1) // 2
    square = gram[...] + taken[:TILE, half:]
    for index in range(planes):
        for block in range(across):
            here = pl.ds((index * across + block) * LANES, LANES)
            total = kept[:, here] + taken[:, here]
            pieces[index, block] = total[:TILE]
            pieces[index, across + block] = total[TILE:]
        pieces[index, tiles - 1] = square


def plane_kernel(arrived, spread):
    total = arrived[0]
    for index in range(1, arrived.shape[0]):
        total += arrived[index]
    for index in range(spread.shape[0]):
        spread[index] = total


def layer_kernel(groups, arrived, spread, gram):
    tiles = spread.shape[1]
    total = arrived[0]
    for index in range(1, arrived.shape[0]):
        total += arrived[index]
    gram[...] = total[tiles] / groups
    for index in range(spread.shape[0]):
        spread[index] = total[:tiles]


def factor_kernel(groups, gram, left, factors):
    rank, rows = left.shape
    shape = (rank, LANES)
    row = lax.broadcasted_iota(jnp.int32, shape, 0)
    col = lax.broadcasted_iota(jnp.int32, shape, 1)
    third = (col >= rank) & (col < 2 * rank)
    square = jnp.concatenate([gram[:, :rank], gram[:, rank : 2 * rank]], axis=0)
    rest = jnp.zeros((rank, LANES - rank - rows), F32)
    table = jnp.concatenate([square, left[...], rest], axis=1)
    table = jnp.concatenate(
        [table[:, :rank], jnp.zeros((rank, rank), F32), table[:, rank : LANES - rank]], axis=1
    )
    table = jnp.where(col == row + rank, 1.0, table)
    roots = jnp.ones((rank, 1), F32)
    for step in range(rank):
        pivot = table[step : step + 1, step : step + 1]
        scaled = table[step : step + 1, :] / pivot
        column = table[:, step : step + 1]
        mine = row[:, :1] == step
        roots = jnp.where(mine, jnp.sqrt(pivot), roots)
        change = jnp.where((row < step) & third, 0.0, column * scaled)
        table = jnp.where(row == step, scaled, table - change)
    table = jnp.where(third, table * roots, table)
    combined = table[:, 2 * rank : 2 * rank + rows].T
    stacked = jnp.concatenate([combined, table[:, rank : 2 * rank]], axis=0) / groups
    high, middle, low = split3(stacked)
    factors[...] = jnp.concatenate([high, high, middle, high, middle, low], axis=1)


def output_kernel(chunks, factors, own, other, base, momentum, new_error, new_momentum, q_next, *scratch):
    error_vmem, momentum_vmem, q_vmem, sems = scratch
    core = lax.axis_index("core")
    rows, cols = base.shape
    half = cols // 2
    across = own.shape[1] // 2
    width = half // chunks
    per = width // (across * LANES)
    copies = []
    for turn, source in enumerate((own, other)):
        begin = (core if turn == 0 else 1 - core) * half
        for chunk in range(chunks):
            parts = []
            for index in range(chunk * per, (chunk + 1) * per):
                for block in range(across):
                    parts.append(jnp.concatenate([source[index, block], source[index, across + block]], axis=0))
            high, middle, low = split3(jnp.concatenate(parts, axis=1))
            depth = jnp.concatenate([high, middle, high, low, middle, high], axis=0)
            product = jnp.dot(factors[...], depth, preferred_element_type=F32)
            approx = product[:rows]
            here = pl.ds(turn * half + chunk * width, width)
            there = pl.ds(pl.multiple_of(begin + chunk * width, LANES), width)
            q_vmem[:, here] = product[rows:]
            error_vmem[:, here] = (base[:, there] - approx).astype(BF16)
            momentum_vmem[:, here] = 0.9 * momentum[:, there] + approx
            for which, (near, far) in enumerate(
                ((error_vmem, new_error), (momentum_vmem, new_momentum), (q_vmem, q_next))
            ):
                copy = pltpu.make_async_copy(
                    near.at[:, here], far.at[:, there], sems.at[which, turn * chunks + chunk]
                )
                copy.start()
                copies.append(copy)
    for copy in copies:
        copy.wait()


def params(megabytes):
    return pltpu.CompilerParams(vmem_limit_bytes=megabytes * 1024 * 1024)


def cost(flops, moved):
    return pl.CostEstimate(flops=flops, bytes_accessed=moved, transcendentals=0)


def shards(grad, error, momentum, q_start):
    groups = lax.axis_size("dp")
    planes = groups * lax.axis_size("x")
    layers = lax.axis_size("z")
    cols, rank = q_start.shape
    rows = grad.shape[1]
    half = cols // 2
    tiles = rank * half // planes // (TILE * LANES)
    swap = [(0, 1), (1, 0)]
    chunk = cols // 6

    term, merged, base = pl.pallas_call(
        functools.partial(left_kernel, chunk),
        out_shape=(
            pltpu.VMEM((rank, rows), F32),
            pltpu.VMEM((rows, cols), BF16),
            pltpu.VMEM((rows, cols), F32),
        ),
        in_specs=[FAR] * 3,
        out_specs=(WHOLE,) * 3,
        scratch_shapes=[
            pltpu.VMEM((rows, cols), BF16),
            pltpu.VMEM((rows, cols), BF16),
            pltpu.VMEM((rank, cols), F32),
            pltpu.SemaphoreType.DMA((3, cols // chunk)),
        ],
        compiler_params=params(58),
        name="left_term",
    )(grad[0], error[0], q_start.T)
    two, three, one = (
        lax.ppermute(term, "dp", [(i, (i + k) % groups) for i in range(groups)]) for k in (1, 3, 2)
    )
    one, two = two, one
    given, gram, left = pl.pallas_call(
        given_kernel,
        out_shape=(
            pltpu.VMEM((rank, half + LANES), F32),
            pltpu.VMEM((TILE, LANES), F32),
            pltpu.VMEM((rank, rows), F32),
        ),
        in_specs=[WHOLE] * 5,
        out_specs=(WHOLE,) * 3,
        compiler_params=params(8),
        name="right_given",
    )(term, one, two, three, merged)
    taken = lax.ppermute(given, "core", swap)
    kept = pl.pallas_call(
        kept_kernel,
        out_shape=pltpu.VMEM((rank, half), F32),
        in_specs=[WHOLE] * 2,
        out_specs=WHOLE,
        compiler_params=params(8),
        cost_estimate=cost(2 * rank * rows * half, 4 * rows * half),
        name="right_kept",
    )(left, merged)
    pieces = pl.pallas_call(
        pieces_kernel,
        out_shape=pltpu.VMEM((planes, tiles + 1, TILE, LANES), F32),
        in_specs=[WHOLE] * 3,
        out_specs=WHOLE,
        compiler_params=params(8),
        name="right_pieces",
    )(kept, gram, taken)
    arrived = lax.all_to_all(pieces, ("dp", "x"), 0, 0)
    spread = pl.pallas_call(
        plane_kernel,
        out_shape=pltpu.VMEM((layers, tiles + 1, TILE, LANES), F32),
        in_specs=[WHOLE],
        out_specs=WHOLE,
        compiler_params=params(8),
        name="plane_sum",
    )(arrived)
    arrived = lax.all_to_all(spread, "z", 0, 0)
    spread, gram = pl.pallas_call(
        functools.partial(layer_kernel, groups),
        out_shape=(pltpu.VMEM((planes, tiles, TILE, LANES), F32), pltpu.VMEM((TILE, LANES), F32)),
        in_specs=[WHOLE],
        out_specs=(WHOLE,) * 2,
        compiler_params=params(8),
        name="layer_sum",
    )(arrived)
    own = lax.all_to_all(spread, ("dp", "x"), 0, 0)
    factors = pl.pallas_call(
        functools.partial(factor_kernel, groups),
        out_shape=pltpu.VMEM((rows + rank, 6 * rank), BF16),
        in_specs=[WHOLE] * 2,
        out_specs=WHOLE,
        compiler_params=params(8),
        cost_estimate=cost(8 * rank * rows * LANES, 4 * rows * LANES),
        name="factors",
    )(gram, left)
    other = lax.ppermute(own, "core", swap)

    chunks = 4
    shapes = (((rows, cols), BF16), ((rows, cols), F32), ((rank, cols), F32))
    new_error, new_momentum, q_next = pl.pallas_call(
        functools.partial(output_kernel, chunks),
        out_shape=tuple(jax.ShapeDtypeStruct(shape, dtype) for shape, dtype in shapes),
        in_specs=[WHOLE] * 5,
        out_specs=(FAR,) * 3,
        scratch_shapes=[pltpu.VMEM(shape, dtype) for shape, dtype in shapes]
        + [pltpu.SemaphoreType.DMA((3, 2 * chunks))],
        compiler_params=params(16),
        name="outputs",
    )(factors, own, other, base, momentum)
    return (new_error[None], new_momentum, q_next.T)


def solution(mesh):
    shape = mesh.shape
    fine = Mesh(mesh.devices.reshape(shape["dp"], 4, 8, 2), ("dp", "x", "z", "core"))
    rows = ("x", "z", "core")
    placed = (P("dp", rows, None), P("dp", rows, None), P(rows, None), P())
    return jax.shard_map(
        shards,
        mesh=fine,
        in_specs=placed,
        out_specs=(P("dp", rows, None), P(rows, None), P()),
        check_vma=False,
    )
```

```python
import functools
import jax
import jax.numpy as jnp
from jax import lax
from jax.experimental import pallas as pl
from jax.experimental.pallas import tpu as pltpu
from jax.sharding import Mesh, PartitionSpec as P

HIGHEST = lax.Precision.HIGHEST
F32 = jnp.float32
BF16 = jnp.bfloat16
LANES = 128
TILE = 8
WHOLE = pl.BlockSpec(memory_space=pltpu.VMEM)
FAR = pl.BlockSpec(memory_space=pltpu.HBM)


def split3(value):
    high = value.astype(BF16)
    rest = value - high.astype(F32)
    middle = rest.astype(BF16)
    low = (rest - middle.astype(F32)).astype(BF16)
    return high, middle, low


def nt_dot(first, second, precision=None):
    return lax.dot_general(
        first, second, (((1,), (1,)), ((), ())), precision=precision, preferred_element_type=F32
    )


def left_kernel(chunk, grad, error, q_start, term, merged, base, grad_vmem, error_vmem, q_vmem, sems):
    count = grad.shape[1] // chunk
    copies = []
    for step in range(count):
        here = pl.ds(step * chunk, chunk)
        group = [
            pltpu.make_async_copy(far.at[:, here], near.at[:, here], sems.at[which, step])
            for which, (far, near) in enumerate(
                ((grad, grad_vmem), (error, error_vmem), (q_start, q_vmem))
            )
        ]
        for copy in group:
            copy.start()
        copies.append(group)
    total = jnp.zeros(term.shape, F32)
    for step in range(count):
        for copy in copies[step]:
            copy.wait()
        here = pl.ds(step * chunk, chunk)
        summed = grad_vmem[:, here].astype(F32) + error_vmem[:, here].astype(F32)
        base[:, here] = summed
        low = summed.astype(BF16)
        merged[:, here] = low
        total += nt_dot(q_vmem[:, here].astype(BF16), low)
    term[...] = total


def given_kernel(term, one, two, three, merged, given, gram, left):
    half = merged.shape[1] // 2
    rank = term.shape[0]
    total = (term[...] + two[...]) + (one[...] + three[...])
    left[...] = total
    there = pl.ds(pl.multiple_of((1 - lax.axis_index("core")) * half, LANES), half)
    given[:, :half] = jnp.dot(total.astype(BF16), merged[:, there], preferred_element_type=F32)
    square = nt_dot(total, total, HIGHEST)
    rest = jnp.zeros((TILE, LANES - 2 * rank), F32)
    tile = jnp.concatenate([square[:TILE], square[TILE:], rest], axis=1)
    gram[...] = tile
    given[:TILE, half:] = tile
    given[TILE:, half:] = jnp.zeros((rank - TILE, LANES), F32)


def kept_kernel(left, merged, momentum, kept, momentum_near, sem):
    copy = pltpu.make_async_copy(momentum, momentum_near, sem)
    copy.start()
    half = merged.shape[1] // 2
    here = pl.ds(pl.multiple_of(lax.axis_index("core") * half, LANES), half)
    kept[...] = jnp.dot(left[...].astype(BF16), merged[:, here], preferred_element_type=F32)
    copy.wait()


def pieces_kernel(kept, gram, taken, pieces):
    half = kept.shape[1]
    planes, tiles = pieces.shape[:2]
    across = (tiles - 1) // 2
    square = gram[...] + taken[:TILE, half:]
    for index in range(planes):
        for block in range(across):
            here = pl.ds((index * across + block) * LANES, LANES)
            total = kept[:, here] + taken[:, here]
            pieces[index, block] = total[:TILE]
            pieces[index, across + block] = total[TILE:]
        pieces[index, tiles - 1] = square


def plane_kernel(arrived, spread):
    total = arrived[0]
    for index in range(1, arrived.shape[0]):
        total += arrived[index]
    for index in range(spread.shape[0]):
        spread[index] = total


def layer_kernel(groups, arrived, spread, gram):
    tiles = spread.shape[1]
    total = arrived[0]
    for index in range(1, arrived.shape[0]):
        total += arrived[index]
    gram[...] = total[tiles] / groups
    for index in range(spread.shape[0]):
        spread[index] = total[:tiles]


def factor_kernel(groups, gram, left, factors):
    rank, rows = left.shape
    shape = (rank, LANES)
    row = lax.broadcasted_iota(jnp.int32, shape, 0)
    col = lax.broadcasted_iota(jnp.int32, shape, 1)
    third = (col >= rank) & (col < 2 * rank)
    square = jnp.concatenate([gram[:, :rank], gram[:, rank : 2 * rank]], axis=0)
    rest = jnp.zeros((rank, LANES - rank - rows), F32)
    table = jnp.concatenate([square, left[...], rest], axis=1)
    table = jnp.concatenate(
        [table[:, :rank], jnp.zeros((rank, rank), F32), table[:, rank : LANES - rank]], axis=1
    )
    table = jnp.where(col == row + rank, 1.0, table)
    roots = jnp.ones((rank, 1), F32)
    for step in range(rank):
        pivot = table[step : step + 1, step : step + 1]
        scaled = table[step : step + 1, :] / pivot
        column = table[:, step : step + 1]
        mine = row[:, :1] == step
        roots = jnp.where(mine, jnp.sqrt(pivot), roots)
        change = jnp.where((row < step) & third, 0.0, column * scaled)
        table = jnp.where(row == step, scaled, table - change)
    table = jnp.where(third, table * roots, table)
    combined = table[:, 2 * rank : 2 * rank + rows].T
    stacked = jnp.concatenate([combined, table[:, rank : 2 * rank]], axis=0) / groups
    high, middle, low = split3(stacked)
    factors[...] = jnp.concatenate([high, high, middle, high, middle, low], axis=1)


def output_kernel(chunks, factors, own, other, base, momentum, new_error, new_momentum, q_next, *scratch):
    error_vmem, momentum_vmem, q_vmem, sems = scratch
    core = lax.axis_index("core")
    rows, cols = base.shape
    half = cols // 2
    across = own.shape[1] // 2
    width = half // chunks
    per = width // (across * LANES)
    copies = []
    for turn, source in enumerate((own, other)):
        begin = (core if turn == 0 else 1 - core) * half
        for chunk in range(chunks):
            parts = []
            for index in range(chunk * per, (chunk + 1) * per):
                for block in range(across):
                    parts.append(jnp.concatenate([source[index, block], source[index, across + block]], axis=0))
            high, middle, low = split3(jnp.concatenate(parts, axis=1))
            depth = jnp.concatenate([high, middle, high, low, middle, high], axis=0)
            product = jnp.dot(factors[...], depth, preferred_element_type=F32)
            approx = product[:rows]
            here = pl.ds(turn * half + chunk * width, width)
            there = pl.ds(pl.multiple_of(begin + chunk * width, LANES), width)
            q_vmem[:, here] = product[rows:]
            error_vmem[:, here] = (base[:, there] - approx).astype(BF16)
            momentum_vmem[:, here] = 0.9 * momentum[:, there] + approx
            for which, (near, far) in enumerate(
                ((error_vmem, new_error), (momentum_vmem, new_momentum), (q_vmem, q_next))
            ):
                copy = pltpu.make_async_copy(
                    near.at[:, here], far.at[:, there], sems.at[which, turn * chunks + chunk]
                )
                copy.start()
                copies.append(copy)
    for copy in copies:
        copy.wait()


def params(megabytes):
    return pltpu.CompilerParams(vmem_limit_bytes=megabytes * 1024 * 1024)


def cost(flops, moved):
    return pl.CostEstimate(flops=flops, bytes_accessed=moved, transcendentals=0)


def shards(grad, error, momentum, q_start):
    groups = lax.axis_size("dp")
    planes = groups * lax.axis_size("x")
    layers = lax.axis_size("z")
    cols, rank = q_start.shape
    rows = grad.shape[1]
    half = cols // 2
    tiles = rank * half // planes // (TILE * LANES)
    swap = [(0, 1), (1, 0)]
    chunk = cols // 6

    term, merged, base = pl.pallas_call(
        functools.partial(left_kernel, chunk),
        out_shape=(
            pltpu.VMEM((rank, rows), F32),
            pltpu.VMEM((rows, cols), BF16),
            pltpu.VMEM((rows, cols), F32),
        ),
        in_specs=[FAR] * 3,
        out_specs=(WHOLE,) * 3,
        scratch_shapes=[
            pltpu.VMEM((rows, cols), BF16),
            pltpu.VMEM((rows, cols), BF16),
            pltpu.VMEM((rank, cols), F32),
            pltpu.SemaphoreType.DMA((3, cols // chunk)),
        ],
        compiler_params=params(58),
        name="left_term",
    )(grad[0], error[0], q_start.T)
    two, three, one = (
        lax.ppermute(term, "dp", [(i, (i + k) % groups) for i in range(groups)]) for k in (1, 3, 2)
    )
    one, two = two, one
    given, gram, left = pl.pallas_call(
        given_kernel,
        out_shape=(
            pltpu.VMEM((rank, half + LANES), F32),
            pltpu.VMEM((TILE, LANES), F32),
            pltpu.VMEM((rank, rows), F32),
        ),
        in_specs=[WHOLE] * 5,
        out_specs=(WHOLE,) * 3,
        compiler_params=params(8),
        name="right_given",
    )(term, one, two, three, merged)
    taken = lax.ppermute(given, "core", swap)
    kept, momentum = pl.pallas_call(
        kept_kernel,
        out_shape=(pltpu.VMEM((rank, half), F32), pltpu.VMEM((rows, cols), F32)),
        in_specs=[WHOLE] * 2 + [FAR],
        out_specs=(WHOLE,) * 2,
        scratch_shapes=[pltpu.SemaphoreType.DMA],
        compiler_params=params(48),
        cost_estimate=cost(2 * rank * rows * half, 4 * rows * cols),
        name="right_kept",
    )(left, merged, momentum)
    pieces = pl.pallas_call(
        pieces_kernel,
        out_shape=pltpu.VMEM((planes, tiles + 1, TILE, LANES), F32),
        in_specs=[WHOLE] * 3,
        out_specs=WHOLE,
        compiler_params=params(8),
        name="right_pieces",
    )(kept, gram, taken)
    arrived = lax.all_to_all(pieces, ("dp", "x"), 0, 0)
    spread = pl.pallas_call(
        plane_kernel,
        out_shape=pltpu.VMEM((layers, tiles + 1, TILE, LANES), F32),
        in_specs=[WHOLE],
        out_specs=WHOLE,
        compiler_params=params(8),
        name="plane_sum",
    )(arrived)
    arrived = lax.all_to_all(spread, "z", 0, 0)
    spread, gram = pl.pallas_call(
        functools.partial(layer_kernel, groups),
        out_shape=(pltpu.VMEM((planes, tiles, TILE, LANES), F32), pltpu.VMEM((TILE, LANES), F32)),
        in_specs=[WHOLE],
        out_specs=(WHOLE,) * 2,
        compiler_params=params(8),
        name="layer_sum",
    )(arrived)
    own = lax.all_to_all(spread, ("dp", "x"), 0, 0)
    factors = pl.pallas_call(
        functools.partial(factor_kernel, groups),
        out_shape=pltpu.VMEM((rows + rank, 6 * rank), BF16),
        in_specs=[WHOLE] * 2,
        out_specs=WHOLE,
        compiler_params=params(8),
        cost_estimate=cost(8 * rank * rows * LANES, 4 * rows * LANES),
        name="factors",
    )(gram, left)
    other = lax.ppermute(own, "core", swap)

    chunks = 4
    shapes = (((rows, cols), BF16), ((rows, cols), F32), ((rank, cols), F32))
    new_error, new_momentum, q_next = pl.pallas_call(
        functools.partial(output_kernel, chunks),
        out_shape=tuple(jax.ShapeDtypeStruct(shape, dtype) for shape, dtype in shapes),
        in_specs=[WHOLE] * 5,
        out_specs=(FAR,) * 3,
        scratch_shapes=[pltpu.VMEM(shape, dtype) for shape, dtype in shapes]
        + [pltpu.SemaphoreType.DMA((3, 2 * chunks))],
        compiler_params=params(16),
        name="outputs",
    )(factors, own, other, base, momentum)
    return (new_error[None], new_momentum, q_next.T)


def solution(mesh):
    shape = mesh.shape
    fine = Mesh(mesh.devices.reshape(shape["dp"], 4, 8, 2), ("dp", "x", "z", "core"))
    rows = ("x", "z", "core")
    placed = (P("dp", rows, None), P("dp", rows, None), P(rows, None), P())
    return jax.shard_map(
        shards,
        mesh=fine,
        in_specs=placed,
        out_specs=(P("dp", rows, None), P(rows, None), P()),
        check_vma=False,
    )
```

```python
import functools
import jax
import jax.numpy as jnp
from jax import lax
from jax.experimental import pallas as pl
from jax.experimental.pallas import tpu as pltpu
from jax.sharding import Mesh, PartitionSpec as P

HIGHEST = lax.Precision.HIGHEST
F32 = jnp.float32
BF16 = jnp.bfloat16
LANES = 128
TILE = 8
WHOLE = pl.BlockSpec(memory_space=pltpu.VMEM)
FAR = pl.BlockSpec(memory_space=pltpu.HBM)


def split3(value):
    high = value.astype(BF16)
    rest = value - high.astype(F32)
    middle = rest.astype(BF16)
    low = (rest - middle.astype(F32)).astype(BF16)
    return high, middle, low


def nt_dot(first, second, precision=None):
    return lax.dot_general(
        first, second, (((1,), (1,)), ((), ())), precision=precision, preferred_element_type=F32
    )


def left_kernel(chunk, grad, error, q_start, term, merged, base, grad_vmem, error_vmem, q_vmem, sems):
    count = grad.shape[1] // chunk
    copies = []
    for step in range(count):
        here = pl.ds(step * chunk, chunk)
        group = [
            pltpu.make_async_copy(far.at[:, here], near.at[:, here], sems.at[which, step])
            for which, (far, near) in enumerate(
                ((grad, grad_vmem), (error, error_vmem), (q_start, q_vmem))
            )
        ]
        for copy in group:
            copy.start()
        copies.append(group)
    total = jnp.zeros(term.shape, F32)
    for step in range(count):
        for copy in copies[step]:
            copy.wait()
        here = pl.ds(step * chunk, chunk)
        summed = grad_vmem[:, here].astype(F32) + error_vmem[:, here].astype(F32)
        base[:, here] = summed
        low = summed.astype(BF16)
        merged[:, here] = low
        total += nt_dot(q_vmem[:, here].astype(BF16), low)
    term[...] = total


def on_core(core, which, run):
    pl.when(core == which)(run)


def bounds(cols, core):
    cut = cols // 3
    return (0, cut) if core == 0 else (cut, cols - cut)


def given_kernel(term, one, two, three, merged, given, gram, left):
    rank = term.shape[0]
    cols = merged.shape[1]
    wide = given.shape[1] - LANES
    total = (term[...] + two[...]) + (one[...] + three[...])
    left[...] = total
    for core in (0, 1):

        def run(core=core):
            begin, count = bounds(cols, 1 - core)
            given[:, :count] = jnp.dot(
                total.astype(BF16), merged[:, pl.ds(begin, count)], preferred_element_type=F32
            )
            if count < wide:
                given[:, pl.ds(count, wide - count)] = jnp.zeros((rank, wide - count), F32)

        on_core(lax.axis_index("core"), core, run)
    square = nt_dot(total, total, HIGHEST)
    rest = jnp.zeros((TILE, LANES - 2 * rank), F32)
    tile = jnp.concatenate([square[:TILE], square[TILE:], rest], axis=1)
    gram[...] = tile
    given[:TILE, wide:] = tile
    given[TILE:, wide:] = jnp.zeros((rank - TILE, LANES), F32)


def kept_kernel(left, merged, kept):
    cols = merged.shape[1]
    for core in (0, 1):

        def run(core=core):
            begin, count = bounds(cols, core)
            kept[:, :count] = jnp.dot(
                left[...].astype(BF16), merged[:, pl.ds(begin, count)], preferred_element_type=F32
            )
            if count < kept.shape[1]:
                kept[:, count:] = jnp.zeros((kept.shape[0], kept.shape[1] - count), F32)

        on_core(lax.axis_index("core"), core, run)


def pieces_kernel(kept, gram, taken, pieces):
    wide = kept.shape[1]
    planes, tiles = pieces.shape[:2]
    across = (tiles - 1) // 2
    square = gram[...] + taken[:TILE, wide:]
    for index in range(planes):
        for block in range(across):
            here = pl.ds((index * across + block) * LANES, LANES)
            total = kept[:, here] + taken[:, here]
            pieces[index, block] = total[:TILE]
            pieces[index, across + block] = total[TILE:]
        pieces[index, tiles - 1] = square


def plane_kernel(arrived, spread):
    total = arrived[0]
    for index in range(1, arrived.shape[0]):
        total += arrived[index]
    for index in range(spread.shape[0]):
        spread[index] = total


def layer_kernel(groups, arrived, spread, gram):
    tiles = spread.shape[1]
    total = arrived[0]
    for index in range(1, arrived.shape[0]):
        total += arrived[index]
    gram[...] = total[tiles] / groups
    for index in range(spread.shape[0]):
        spread[index] = total[:tiles]


def factor_kernel(groups, gram, left, factors):
    rank, rows = left.shape
    shape = (rank, LANES)
    row = lax.broadcasted_iota(jnp.int32, shape, 0)
    col = lax.broadcasted_iota(jnp.int32, shape, 1)
    third = (col >= rank) & (col < 2 * rank)
    square = jnp.concatenate([gram[:, :rank], gram[:, rank : 2 * rank]], axis=0)
    rest = jnp.zeros((rank, LANES - rank - rows), F32)
    table = jnp.concatenate([square, left[...], rest], axis=1)
    table = jnp.concatenate(
        [table[:, :rank], jnp.zeros((rank, rank), F32), table[:, rank : LANES - rank]], axis=1
    )
    table = jnp.where(col == row + rank, 1.0, table)
    roots = jnp.ones((rank, 1), F32)
    for step in range(rank):
        pivot = table[step : step + 1, step : step + 1]
        scaled = table[step : step + 1, :] / pivot
        column = table[:, step : step + 1]
        mine = row[:, :1] == step
        roots = jnp.where(mine, jnp.sqrt(pivot), roots)
        change = jnp.where((row < step) & third, 0.0, column * scaled)
        table = jnp.where(row == step, scaled, table - change)
    table = jnp.where(third, table * roots, table)
    combined = table[:, 2 * rank : 2 * rank + rows].T
    stacked = jnp.concatenate([combined, table[:, rank : 2 * rank]], axis=0) / groups
    high, middle, low = split3(stacked)
    factors[...] = jnp.concatenate([high, high, middle, high, middle, low], axis=1)


def pad_kernel(arrived, own):
    count = arrived.shape[0]
    own[:count] = arrived[...]
    own[count:] = jnp.zeros((own.shape[0] - count,) + own.shape[1:], F32)


def output_kernel(planes, chunks, factors, own, other, base, momentum, new_error, new_momentum, q_next, *scratch):
    error_vmem, momentum_vmem, q_vmem, sems = scratch
    rows, cols = base.shape
    width = cols // chunks

    def run(sources):
        copies = []
        slabs = []
        for core, source in enumerate(sources):
            begin, count = bounds(cols, core)
            tiles = 2 * count // planes // LANES
            across = tiles // 2
            for index in range(planes):
                for block in range(across):
                    slabs.append((source, index * tiles + block, index * tiles + across + block))
        per = len(slabs) // chunks
        for chunk in range(chunks):
            parts = [
                jnp.concatenate([source[upper], source[lower]], axis=0)
                for source, upper, lower in slabs[chunk * per : (chunk + 1) * per]
            ]
            high, middle, low = split3(jnp.concatenate(parts, axis=1))
            depth = jnp.concatenate([high, middle, high, low, middle, high], axis=0)
            product = jnp.dot(factors[...], depth, preferred_element_type=F32)
            approx = product[:rows]
            here = pl.ds(chunk * width, width)
            q_vmem[:, here] = product[rows:]
            error_vmem[:, here] = (base[:, here] - approx).astype(BF16)
            momentum_vmem[:, here] = 0.9 * momentum[:, here] + approx
            for which, (near, far) in enumerate(
                ((error_vmem, new_error), (momentum_vmem, new_momentum), (q_vmem, q_next))
            ):
                copy = pltpu.make_async_copy(near.at[:, here], far.at[:, here], sems.at[which, chunk])
                copy.start()
                copies.append(copy)
        for copy in copies:
            copy.wait()

    core = lax.axis_index("core")
    on_core(core, 0, lambda: run((own, other)))
    on_core(core, 1, lambda: run((other, own)))


def params(megabytes):
    return pltpu.CompilerParams(vmem_limit_bytes=megabytes * 1024 * 1024)


def cost(flops, moved):
    return pl.CostEstimate(flops=flops, bytes_accessed=moved, transcendentals=0)


def shards(grad, error, momentum, q_start):
    groups = lax.axis_size("dp")
    planes = groups * lax.axis_size("x")
    layers = lax.axis_size("z")
    cols, rank = q_start.shape
    rows = grad.shape[1]
    wide = bounds(cols, 1)[1]
    swap = [(0, 1), (1, 0)]
    chunk = cols // 6

    def call(kernel, name, out_shape, *args, **options):
        many = isinstance(out_shape, tuple)
        return pl.pallas_call(
            kernel,
            out_shape=out_shape,
            in_specs=[WHOLE] * len(args),
            out_specs=(WHOLE,) * len(out_shape) if many else WHOLE,
            compiler_params=params(8),
            name=name,
            **options,
        )(*args)

    term, merged, base = pl.pallas_call(
        functools.partial(left_kernel, chunk),
        out_shape=(
            pltpu.VMEM((rank, rows), F32),
            pltpu.VMEM((rows, cols), BF16),
            pltpu.VMEM((rows, cols), F32),
        ),
        in_specs=[FAR] * 3,
        out_specs=(WHOLE,) * 3,
        scratch_shapes=[
            pltpu.VMEM((rows, cols), BF16),
            pltpu.VMEM((rows, cols), BF16),
            pltpu.VMEM((rank, cols), F32),
            pltpu.SemaphoreType.DMA((3, cols // chunk)),
        ],
        compiler_params=params(58),
        name="left_term",
    )(grad[0], error[0], q_start.T)
    three, one, two = (
        lax.ppermute(term, "dp", [(i, (i + k) % groups) for i in range(groups)]) for k in (3, 1, 2)
    )
    given, gram, left = call(
        given_kernel,
        "right_given",
        (
            pltpu.VMEM((rank, wide + LANES), F32),
            pltpu.VMEM((TILE, LANES), F32),
            pltpu.VMEM((rank, rows), F32),
        ),
        term, one, two, three, merged,
    )
    taken = lax.ppermute(given, "core", swap)
    kept = call(
        kept_kernel,
        "right_kept",
        pltpu.VMEM((rank, wide), F32),
        left, merged,
        cost_estimate=cost(2 * rank * rows * wide, 4 * rows * wide),
    )

    def reduced(core):
        count = bounds(cols, core)[1]
        tiles = rank * count // planes // (TILE * LANES)
        full = rank * wide // (TILE * LANES)
        tag = str(core)

        def run(kept, gram, taken):
            shape = (planes, tiles + 1, TILE, LANES)
            pieces = call(pieces_kernel, "pieces" + tag, pltpu.VMEM(shape, F32), kept, gram, taken)
            arrived = lax.all_to_all(pieces, ("dp", "x"), 0, 0)
            shape = (layers, tiles + 1, TILE, LANES)
            spread = call(plane_kernel, "plane_sum" + tag, pltpu.VMEM(shape, F32), arrived)
            arrived = lax.all_to_all(spread, "z", 0, 0)
            shape = (planes, tiles, TILE, LANES)
            spread, square = call(
                functools.partial(layer_kernel, groups),
                "layer_sum" + tag,
                (pltpu.VMEM(shape, F32), pltpu.VMEM((TILE, LANES), F32)),
                arrived,
            )
            own = lax.all_to_all(spread, ("dp", "x"), 0, 0).reshape(planes * tiles, TILE, LANES)
            if planes * tiles < full:
                own = call(pad_kernel, "pad" + tag, pltpu.VMEM((full, TILE, LANES), F32), own)
            return own, square

        return run

    own, gram = lax.cond(lax.axis_index("core") == 0, reduced(0), reduced(1), kept, gram, taken)
    factors = call(
        functools.partial(factor_kernel, groups),
        "factors",
        pltpu.VMEM((rows + rank, 6 * rank), BF16),
        gram, left,
        cost_estimate=cost(8 * rank * rows * LANES, 4 * rows * LANES),
    )
    other = lax.ppermute(own, "core", swap)

    chunks = 8
    shapes = (((rows, cols), BF16), ((rows, cols), F32), ((rank, cols), F32))
    new_error, new_momentum, q_next = pl.pallas_call(
        functools.partial(output_kernel, planes, chunks),
        out_shape=tuple(jax.ShapeDtypeStruct(shape, dtype) for shape, dtype in shapes),
        in_specs=[WHOLE] * 5,
        out_specs=(FAR,) * 3,
        scratch_shapes=[pltpu.VMEM(shape, dtype) for shape, dtype in shapes]
        + [pltpu.SemaphoreType.DMA((3, chunks))],
        compiler_params=params(16),
        name="outputs",
    )(factors, own, other, base, momentum)
    return (new_error[None], new_momentum, q_next.T)


def solution(mesh):
    shape = mesh.shape
    fine = Mesh(mesh.devices.reshape(shape["dp"], 4, 8, 2), ("dp", "x", "z", "core"))
    rows = ("x", "z", "core")
    placed = (P("dp", rows, None), P("dp", rows, None), P(rows, None), P())
    return jax.shard_map(
        shards,
        mesh=fine,
        in_specs=placed,
        out_specs=(P("dp", rows, None), P(rows, None), P()),
        check_vma=False,
    )
```

```python
import functools
import jax
import jax.numpy as jnp
from jax import lax
from jax.experimental import pallas as pl
from jax.experimental.pallas import tpu as pltpu
from jax.sharding import Mesh, PartitionSpec as P

HIGHEST = lax.Precision.HIGHEST
F32 = jnp.float32
BF16 = jnp.bfloat16
LANES = 128
TILE = 8
WHOLE = pl.BlockSpec(memory_space=pltpu.VMEM)
FAR = pl.BlockSpec(memory_space=pltpu.HBM)


def split3(value):
    high = value.astype(BF16)
    rest = value - high.astype(F32)
    middle = rest.astype(BF16)
    low = (rest - middle.astype(F32)).astype(BF16)
    return high, middle, low


def nt_dot(first, second, precision=None):
    return lax.dot_general(
        first, second, (((1,), (1,)), ((), ())), precision=precision, preferred_element_type=F32
    )


def left_kernel(chunk, grad, error, q_start, term, merged, base, grad_vmem, error_vmem, q_vmem, sems):
    count = grad.shape[1] // chunk
    copies = []
    for step in range(count):
        here = pl.ds(step * chunk, chunk)
        group = [
            pltpu.make_async_copy(far.at[:, here], near.at[:, here], sems.at[which, step])
            for which, (far, near) in enumerate(
                ((grad, grad_vmem), (error, error_vmem), (q_start, q_vmem))
            )
        ]
        for copy in group:
            copy.start()
        copies.append(group)
    total = jnp.zeros(term.shape, F32)
    for step in range(count):
        for copy in copies[step]:
            copy.wait()
        here = pl.ds(step * chunk, chunk)
        summed = grad_vmem[:, here].astype(F32) + error_vmem[:, here].astype(F32)
        base[:, here] = summed
        low = summed.astype(BF16)
        merged[:, here] = low
        total += nt_dot(q_vmem[:, here].astype(BF16), low)
    term[...] = total


def given_kernel(term, one, two, three, merged, given, gram, left):
    half = merged.shape[1] // 2
    rank = term.shape[0]
    total = (term[...] + two[...]) + (one[...] + three[...])
    left[...] = total
    there = pl.ds(pl.multiple_of((1 - lax.axis_index("core")) * half, LANES), half)
    given[:, :half] = jnp.dot(total.astype(BF16), merged[:, there], preferred_element_type=F32)
    square = nt_dot(total, total, HIGHEST)
    rest = jnp.zeros((TILE, LANES - 2 * rank), F32)
    tile = jnp.concatenate([square[:TILE], square[TILE:], rest], axis=1)
    gram[...] = tile
    given[:TILE, half:] = tile
    given[TILE:, half:] = jnp.zeros((rank - TILE, LANES), F32)


def kept_kernel(left, merged, kept):
    half = merged.shape[1] // 2
    here = pl.ds(pl.multiple_of(lax.axis_index("core") * half, LANES), half)
    kept[...] = jnp.dot(left[...].astype(BF16), merged[:, here], preferred_element_type=F32)


def pieces_kernel(kept, gram, taken, pieces):
    half = kept.shape[1]
    planes, tiles = pieces.shape[:2]
    across = (tiles - 1) // 2
    square = gram[...] + taken[:TILE, half:]
    for index in range(planes):
        for block in range(across):
            here = pl.ds((index * across + block) * LANES, LANES)
            total = kept[:, here] + taken[:, here]
            pieces[index, block] = total[:TILE]
            pieces[index, across + block] = total[TILE:]
        pieces[index, tiles - 1] = square


def plane_kernel(arrived, spread):
    total = arrived[0]
    for index in range(1, arrived.shape[0]):
        total += arrived[index]
    for index in range(spread.shape[0]):
        spread[index] = total


def layer_kernel(groups, arrived, spread, gram):
    tiles = spread.shape[1]
    total = arrived[0]
    for index in range(1, arrived.shape[0]):
        total += arrived[index]
    gram[...] = total[tiles] / groups
    for index in range(spread.shape[0]):
        spread[index] = total[:tiles]


def make_factors(groups, gram, left, factors):
    rank, rows = left.shape
    shape = (rank, LANES)
    row = lax.broadcasted_iota(jnp.int32, shape, 0)
    col = lax.broadcasted_iota(jnp.int32, shape, 1)
    third = (col >= rank) & (col < 2 * rank)
    square = jnp.concatenate([gram[:, :rank], gram[:, rank : 2 * rank]], axis=0)
    rest = jnp.zeros((rank, LANES - 2 * rank - rows), F32)
    table = jnp.concatenate([square, jnp.zeros((rank, rank), F32), left[...], rest], axis=1)
    table = jnp.where(col == row + rank, 1.0, table)
    roots = jnp.ones((rank, 1), F32)
    for step in range(0, rank, 2):
        after = step + 1
        first = table[step:after, step:after]
        ratio = table[step:after, after : after + 1] / first
        below = table[after : after + 1, step:after]
        second = table[after : after + 1, after : after + 1] - below * ratio
        upper = table[step:after, :] / first
        lower = (table[after : after + 1, :] - below * upper) / second
        column = table[:, step:after]
        beside = table[:, after : after + 1] - column * ratio
        change = jnp.where((row < step) & third, 0.0, column * upper + beside * lower)
        upper = jnp.where(third[:1], upper, upper - ratio * lower)
        table = jnp.where(row == step, upper, jnp.where(row == after, lower, table - change))
        roots = jnp.where(row[:, :1] == step, jnp.sqrt(first), roots)
        roots = jnp.where(row[:, :1] == after, jnp.sqrt(second), roots)
    table = jnp.where(third, table * roots, table)
    combined = table[:, 2 * rank : 2 * rank + rows].T
    stacked = jnp.concatenate([combined, table[:, rank : 2 * rank]], axis=0) / groups
    high, middle, low = split3(stacked)
    factors[...] = jnp.concatenate([high, high, middle, high, middle, low], axis=1)


def put_halves(chunks, halves, factors, base, momentum, outs, scratch):
    error_vmem, momentum_vmem, q_vmem, sems = scratch
    rows, cols = base.shape
    half = cols // 2
    width = half // chunks
    copies = []
    for turn, (begin, source) in enumerate(halves):
        across = source.shape[1] // 2
        per = width // (across * LANES)
        for chunk in range(chunks):
            parts = []
            for index in range(chunk * per, (chunk + 1) * per):
                for block in range(across):
                    parts.append(jnp.concatenate([source[index, block], source[index, across + block]], axis=0))
            high, middle, low = split3(jnp.concatenate(parts, axis=1))
            depth = jnp.concatenate([high, middle, high, low, middle, high], axis=0)
            product = jnp.dot(factors[...], depth, preferred_element_type=F32)
            approx = product[:rows]
            here = pl.ds(turn * half + chunk * width, width)
            there = pl.ds(begin + chunk * width, width)
            q_vmem[:, here] = product[rows:]
            error_vmem[:, here] = (base[:, there] - approx).astype(BF16)
            momentum_vmem[:, here] = 0.9 * momentum[:, there] + approx
            for which, (near, far) in enumerate(zip((error_vmem, momentum_vmem, q_vmem), outs)):
                copy = pltpu.make_async_copy(
                    near.at[:, here], far.at[:, there], sems.at[which, turn * chunks + chunk]
                )
                copy.start()
                copies.append(copy)
    for copy in copies:
        copy.wait()


def ahead_kernel(groups, chunks, gram, left, own, base, momentum, same, factors, *rest):
    same[...] = own[...]

    @pl.when(lax.axis_index("core") == 1)
    def _():
        make_factors(groups, gram, left, factors)
        half = base.shape[1] // 2
        put_halves(chunks, ((half, own),), factors, base, momentum, rest[:3], rest[3:])


def factor_kernel(groups, gram, left, factors):
    @pl.when(lax.axis_index("core") == 0)
    def _():
        make_factors(groups, gram, left, factors)


def output_kernel(chunks, ahead, beside, own, other, base, momentum, *rest):
    outs, scratch = rest[3:6], rest[6:]
    half = base.shape[1] // 2
    core = lax.axis_index("core")

    @pl.when(core == 0)
    def _():
        put_halves(chunks, ((0, own), (half, other)), beside, base, momentum, outs, scratch)

    @pl.when(core == 1)
    def _():
        put_halves(chunks, ((0, other),), ahead, base, momentum, outs, scratch)


def params(megabytes):
    return pltpu.CompilerParams(vmem_limit_bytes=megabytes * 1024 * 1024)


def cost(flops, moved):
    return pl.CostEstimate(flops=flops, bytes_accessed=moved, transcendentals=0)


def shards(grad, error, momentum, q_start):
    groups = lax.axis_size("dp")
    planes = groups * lax.axis_size("x")
    layers = lax.axis_size("z")
    cols, rank = q_start.shape
    rows = grad.shape[1]
    half = cols // 2
    tiles = rank * half // planes // (TILE * LANES)
    swap = [(0, 1), (1, 0)]
    chunk = cols // 6

    term, merged, base = pl.pallas_call(
        functools.partial(left_kernel, chunk),
        out_shape=(
            pltpu.VMEM((rank, rows), F32),
            pltpu.VMEM((rows, cols), BF16),
            pltpu.VMEM((rows, cols), F32),
        ),
        in_specs=[FAR] * 3,
        out_specs=(WHOLE,) * 3,
        scratch_shapes=[
            pltpu.VMEM((rows, cols), BF16),
            pltpu.VMEM((rows, cols), BF16),
            pltpu.VMEM((rank, cols), F32),
            pltpu.SemaphoreType.DMA((3, cols // chunk)),
        ],
        compiler_params=params(58),
        name="left_term",
    )(grad[0], error[0], q_start.T)
    two, three, one = (
        lax.ppermute(term, "dp", [(i, (i + k) % groups) for i in range(groups)]) for k in (1, 3, 2)
    )
    one, two = two, one
    given, gram, left = pl.pallas_call(
        given_kernel,
        out_shape=(
            pltpu.VMEM((rank, half + LANES), F32),
            pltpu.VMEM((TILE, LANES), F32),
            pltpu.VMEM((rank, rows), F32),
        ),
        in_specs=[WHOLE] * 5,
        out_specs=(WHOLE,) * 3,
        compiler_params=params(8),
        name="right_given",
    )(term, one, two, three, merged)
    taken = lax.ppermute(given, "core", swap)
    kept = pl.pallas_call(
        kept_kernel,
        out_shape=pltpu.VMEM((rank, half), F32),
        in_specs=[WHOLE] * 2,
        out_specs=WHOLE,
        compiler_params=params(8),
        cost_estimate=cost(2 * rank * rows * half, 4 * rows * half),
        name="right_kept",
    )(left, merged)
    pieces = pl.pallas_call(
        pieces_kernel,
        out_shape=pltpu.VMEM((planes, tiles + 1, TILE, LANES), F32),
        in_specs=[WHOLE] * 3,
        out_specs=WHOLE,
        compiler_params=params(8),
        name="right_pieces",
    )(kept, gram, taken)
    arrived = lax.all_to_all(pieces, ("dp", "x"), 0, 0)
    spread = pl.pallas_call(
        plane_kernel,
        out_shape=pltpu.VMEM((layers, tiles + 1, TILE, LANES), F32),
        in_specs=[WHOLE],
        out_specs=WHOLE,
        compiler_params=params(8),
        name="plane_sum",
    )(arrived)
    arrived = lax.all_to_all(spread, "z", 0, 0)
    spread, gram = pl.pallas_call(
        functools.partial(layer_kernel, groups),
        out_shape=(pltpu.VMEM((planes, tiles, TILE, LANES), F32), pltpu.VMEM((TILE, LANES), F32)),
        in_specs=[WHOLE],
        out_specs=(WHOLE,) * 2,
        compiler_params=params(8),
        name="layer_sum",
    )(arrived)
    own = lax.all_to_all(spread, ("dp", "x"), 0, 0)
    chunks = 4
    shapes = (((rows, cols), BF16), ((rows, cols), F32), ((rank, cols), F32))
    out_shapes = tuple(jax.ShapeDtypeStruct(shape, dtype) for shape, dtype in shapes)
    factor_shape = pltpu.VMEM((rows + rank, 6 * rank), BF16)

    def scratch(halves):
        buffers = [pltpu.VMEM((shape[0], halves * half), dtype) for shape, dtype in shapes]
        return buffers + [pltpu.SemaphoreType.DMA((3, halves * chunks))]

    own, ahead, *begun = pl.pallas_call(
        functools.partial(ahead_kernel, groups, chunks),
        out_shape=(pltpu.VMEM(own.shape, F32), factor_shape) + out_shapes,
        in_specs=[WHOLE] * 5,
        out_specs=(WHOLE,) * 2 + (FAR,) * 3,
        scratch_shapes=scratch(1),
        compiler_params=params(8),
        name="outputs_ahead",
    )(gram, left, own, base, momentum)
    other = lax.ppermute(own, "core", swap)
    beside = pl.pallas_call(
        functools.partial(factor_kernel, groups),
        out_shape=factor_shape,
        in_specs=[WHOLE] * 2,
        out_specs=WHOLE,
        compiler_params=params(8),
        cost_estimate=cost(8 * rank * rows * LANES, 4 * rows * LANES),
        name="factors",
    )(gram, left)
    new_error, new_momentum, q_next = pl.pallas_call(
        functools.partial(output_kernel, chunks),
        out_shape=out_shapes,
        in_specs=[WHOLE] * 6 + [FAR] * 3,
        out_specs=(FAR,) * 3,
        scratch_shapes=scratch(2),
        input_output_aliases={6: 0, 7: 1, 8: 2},
        compiler_params=params(12),
        name="outputs",
    )(ahead, beside, own, other, base, momentum, *begun)
    return (new_error[None], new_momentum, q_next.T)


def solution(mesh):
    shape = mesh.shape
    fine = Mesh(mesh.devices.reshape(shape["dp"], 4, 8, 2), ("dp", "x", "z", "core"))
    rows = ("x", "z", "core")
    placed = (P("dp", rows, None), P("dp", rows, None), P(rows, None), P())
    return jax.shard_map(
        shards,
        mesh=fine,
        in_specs=placed,
        out_specs=(P("dp", rows, None), P(rows, None), P()),
        check_vma=False,
    )
```

```python
import functools
import jax
import jax.numpy as jnp
from jax import lax
from jax.experimental import pallas as pl
from jax.experimental.pallas import tpu as pltpu
from jax.sharding import Mesh, PartitionSpec as P

HIGHEST = lax.Precision.HIGHEST
F32 = jnp.float32
BF16 = jnp.bfloat16
LANES = 128
TILE = 8
WHOLE = pl.BlockSpec(memory_space=pltpu.VMEM)
FAR = pl.BlockSpec(memory_space=pltpu.HBM)


def split3(value):
    high = value.astype(BF16)
    rest = value - high.astype(F32)
    middle = rest.astype(BF16)
    low = (rest - middle.astype(F32)).astype(BF16)
    return high, middle, low


def nt_dot(first, second, precision=None):
    return lax.dot_general(
        first, second, (((1,), (1,)), ((), ())), precision=precision, preferred_element_type=F32
    )


def left_kernel(parts, grad, error, q_start, term, merged, base, grad_vmem, error_vmem, q_vmem, sems):
    unit = grad.shape[1] // sum(parts)
    slabs = [pl.ds(sum(parts[:step]) * unit, parts[step] * unit) for step in range(len(parts))]
    copies = []
    for step, here in enumerate(slabs):
        group = [
            pltpu.make_async_copy(far.at[:, here], near.at[:, here], sems.at[which, step])
            for which, (far, near) in enumerate(
                ((grad, grad_vmem), (error, error_vmem), (q_start, q_vmem))
            )
        ]
        for copy in group:
            copy.start()
        copies.append(group)
    total = jnp.zeros(term.shape, F32)
    for group, here in zip(copies, slabs):
        for copy in group:
            copy.wait()
        summed = grad_vmem[:, here].astype(F32) + error_vmem[:, here].astype(F32)
        base[:, here] = summed
        low = summed.astype(BF16)
        merged[:, here] = low
        total += nt_dot(q_vmem[:, here].astype(BF16), low)
    term[...] = total


def given_kernel(term, one, two, three, merged, given, gram, left):
    half = merged.shape[1] // 2
    rank = term.shape[0]
    total = (term[...] + two[...]) + (one[...] + three[...])
    left[...] = total
    there = pl.ds(pl.multiple_of((1 - lax.axis_index("core")) * half, LANES), half)
    given[:, :half] = jnp.dot(total.astype(BF16), merged[:, there], preferred_element_type=F32)
    square = nt_dot(total, total, HIGHEST)
    rest = jnp.zeros((TILE, LANES - 2 * rank), F32)
    tile = jnp.concatenate([square[:TILE], square[TILE:], rest], axis=1)
    gram[...] = tile
    given[:TILE, half:] = tile
    given[TILE:, half:] = jnp.zeros((rank - TILE, LANES), F32)


def kept_kernel(left, merged, kept):
    half = merged.shape[1] // 2
    here = pl.ds(pl.multiple_of(lax.axis_index("core") * half, LANES), half)
    kept[...] = jnp.dot(left[...].astype(BF16), merged[:, here], preferred_element_type=F32)


def pieces_kernel(kept, gram, taken, pieces):
    half = kept.shape[1]
    planes, tiles = pieces.shape[:2]
    across = (tiles - 1) // 2
    square = gram[...] + taken[:TILE, half:]
    for index in range(planes):
        for block in range(across):
            here = pl.ds((index * across + block) * LANES, LANES)
            total = kept[:, here] + taken[:, here]
            pieces[index, block] = total[:TILE]
            pieces[index, across + block] = total[TILE:]
        pieces[index, tiles - 1] = square


def plane_kernel(arrived, spread):
    total = arrived[0]
    for index in range(1, arrived.shape[0]):
        total += arrived[index]
    for index in range(spread.shape[0]):
        spread[index] = total


def layer_kernel(groups, arrived, spread, gram):
    tiles = spread.shape[1]
    total = arrived[0]
    for index in range(1, arrived.shape[0]):
        total += arrived[index]
    gram[...] = total[tiles] / groups
    for index in range(spread.shape[0]):
        spread[index] = total[:tiles]


def make_factors(groups, gram, left, factors):
    rank, rows = left.shape
    shape = (rank, LANES)
    row = lax.broadcasted_iota(jnp.int32, shape, 0)
    col = lax.broadcasted_iota(jnp.int32, shape, 1)
    third = (col >= rank) & (col < 2 * rank)
    square = jnp.concatenate([gram[:, :rank], gram[:, rank : 2 * rank]], axis=0)
    rest = jnp.zeros((rank, LANES - 2 * rank - rows), F32)
    table = jnp.concatenate([square, jnp.zeros((rank, rank), F32), left[...], rest], axis=1)
    table = jnp.where(col == row + rank, 1.0, table)
    pivots = jnp.ones(shape, F32)
    for step in range(rank):
        column = jnp.broadcast_to(table[:, step : step + 1], shape)
        scaled = table[step : step + 1, :] / column[step : step + 1, :]
        pivots = jnp.where(row == step, column, pivots)
        change = jnp.where((row < step) & third, 0.0, column * scaled)
        table = jnp.where(row == step, scaled, table - change)
    table = jnp.where(third, table * jnp.sqrt(pivots), table)
    combined = table[:, 2 * rank : 2 * rank + rows].T
    stacked = jnp.concatenate([combined, table[:, rank : 2 * rank]], axis=0) / groups
    high, middle, low = split3(stacked)
    factors[...] = jnp.concatenate([high, high, middle, high, middle, low], axis=1)


def put_halves(chunks, halves, factors, base, momentum, outs, scratch):
    error_vmem, momentum_vmem, q_vmem, sems = scratch
    rows, cols = base.shape
    half = cols // 2
    width = half // chunks
    copies = []
    for turn, (begin, source) in enumerate(halves):
        across = source.shape[1] // 2
        per = width // (across * LANES)
        for chunk in range(chunks):
            parts = []
            for index in range(chunk * per, (chunk + 1) * per):
                for block in range(across):
                    parts.append(jnp.concatenate([source[index, block], source[index, across + block]], axis=0))
            high, middle, low = split3(jnp.concatenate(parts, axis=1))
            depth = jnp.concatenate([high, middle, high, low, middle, high], axis=0)
            product = jnp.dot(factors[...], depth, preferred_element_type=F32)
            approx = product[:rows]
            here = pl.ds(turn * half + chunk * width, width)
            there = pl.ds(begin + chunk * width, width)
            q_vmem[:, here] = product[rows:]
            error_vmem[:, here] = (base[:, there] - approx).astype(BF16)
            momentum_vmem[:, here] = 0.9 * momentum[:, there] + approx
            for which, (near, far) in enumerate(zip((error_vmem, momentum_vmem, q_vmem), outs)):
                copy = pltpu.make_async_copy(
                    near.at[:, here], far.at[:, there], sems.at[which, turn * chunks + chunk]
                )
                copy.start()
                copies.append(copy)
    for copy in copies:
        copy.wait()


def ahead_kernel(groups, chunks, gram, left, own, base, momentum, same, factors, *rest):
    same[...] = own[...]

    @pl.when(lax.axis_index("core") == 1)
    def _():
        make_factors(groups, gram, left, factors)
        half = base.shape[1] // 2
        put_halves(chunks, ((half, own),), factors, base, momentum, rest[:3], rest[3:])


def factor_kernel(groups, gram, left, factors):
    @pl.when(lax.axis_index("core") == 0)
    def _():
        make_factors(groups, gram, left, factors)


def output_kernel(chunks, ahead, beside, own, other, base, momentum, *rest):
    outs, scratch = rest[3:6], rest[6:]
    half = base.shape[1] // 2
    core = lax.axis_index("core")

    @pl.when(core == 0)
    def _():
        put_halves(chunks, ((0, own), (half, other)), beside, base, momentum, outs, scratch)

    @pl.when(core == 1)
    def _():
        put_halves(chunks, ((0, other),), ahead, base, momentum, outs, scratch)


def params(megabytes):
    return pltpu.CompilerParams(vmem_limit_bytes=megabytes * 1024 * 1024)


def cost(flops, moved):
    return pl.CostEstimate(flops=flops, bytes_accessed=moved, transcendentals=0)


def shards(grad, error, momentum, q_start):
    groups = lax.axis_size("dp")
    planes = groups * lax.axis_size("x")
    layers = lax.axis_size("z")
    cols, rank = q_start.shape
    rows = grad.shape[1]
    half = cols // 2
    tiles = rank * half // planes // (TILE * LANES)
    swap = [(0, 1), (1, 0)]
    parts = (5, 4, 2, 1)

    term, merged, base = pl.pallas_call(
        functools.partial(left_kernel, parts),
        out_shape=(
            pltpu.VMEM((rank, rows), F32),
            pltpu.VMEM((rows, cols), BF16),
            pltpu.VMEM((rows, cols), F32),
        ),
        in_specs=[FAR] * 3,
        out_specs=(WHOLE,) * 3,
        scratch_shapes=[
            pltpu.VMEM((rows, cols), BF16),
            pltpu.VMEM((rows, cols), BF16),
            pltpu.VMEM((rank, cols), F32),
            pltpu.SemaphoreType.DMA((3, len(parts))),
        ],
        compiler_params=params(58),
        name="left_term",
    )(grad[0], error[0], q_start.T)
    two, three, one = (
        lax.ppermute(term, "dp", [(i, (i + k) % groups) for i in range(groups)]) for k in (1, 3, 2)
    )
    one, two = two, one
    given, gram, left = pl.pallas_call(
        given_kernel,
        out_shape=(
            pltpu.VMEM((rank, half + LANES), F32),
            pltpu.VMEM((TILE, LANES), F32),
            pltpu.VMEM((rank, rows), F32),
        ),
        in_specs=[WHOLE] * 5,
        out_specs=(WHOLE,) * 3,
        compiler_params=params(8),
        name="right_given",
    )(term, one, two, three, merged)
    taken = lax.ppermute(given, "core", swap)
    kept = pl.pallas_call(
        kept_kernel,
        out_shape=pltpu.VMEM((rank, half), F32),
        in_specs=[WHOLE] * 2,
        out_specs=WHOLE,
        compiler_params=params(8),
        cost_estimate=cost(2 * rank * rows * half, 4 * rows * half),
        name="right_kept",
    )(left, merged)
    pieces = pl.pallas_call(
        pieces_kernel,
        out_shape=pltpu.VMEM((planes, tiles + 1, TILE, LANES), F32),
        in_specs=[WHOLE] * 3,
        out_specs=WHOLE,
        compiler_params=params(8),
        name="right_pieces",
    )(kept, gram, taken)
    arrived = lax.all_to_all(pieces, ("dp", "x"), 0, 0)
    spread = pl.pallas_call(
        plane_kernel,
        out_shape=pltpu.VMEM((layers, tiles + 1, TILE, LANES), F32),
        in_specs=[WHOLE],
        out_specs=WHOLE,
        compiler_params=params(8),
        name="plane_sum",
    )(arrived)
    arrived = lax.all_to_all(spread, "z", 0, 0)
    spread, gram = pl.pallas_call(
        functools.partial(layer_kernel, groups),
        out_shape=(pltpu.VMEM((planes, tiles, TILE, LANES), F32), pltpu.VMEM((TILE, LANES), F32)),
        in_specs=[WHOLE],
        out_specs=(WHOLE,) * 2,
        compiler_params=params(8),
        name="layer_sum",
    )(arrived)
    own = lax.all_to_all(spread, ("dp", "x"), 0, 0)
    chunks = 4
    shapes = (((rows, cols), BF16), ((rows, cols), F32), ((rank, cols), F32))
    out_shapes = tuple(jax.ShapeDtypeStruct(shape, dtype) for shape, dtype in shapes)
    factor_shape = pltpu.VMEM((rows + rank, 6 * rank), BF16)

    def scratch(halves):
        buffers = [pltpu.VMEM((shape[0], halves * half), dtype) for shape, dtype in shapes]
        return buffers + [pltpu.SemaphoreType.DMA((3, halves * chunks))]

    own, ahead, *begun = pl.pallas_call(
        functools.partial(ahead_kernel, groups, chunks),
        out_shape=(pltpu.VMEM(own.shape, F32), factor_shape) + out_shapes,
        in_specs=[WHOLE] * 5,
        out_specs=(WHOLE,) * 2 + (FAR,) * 3,
        scratch_shapes=scratch(1),
        compiler_params=params(8),
        name="outputs_ahead",
    )(gram, left, own, base, momentum)
    other = lax.ppermute(own, "core", swap)
    beside = pl.pallas_call(
        functools.partial(factor_kernel, groups),
        out_shape=factor_shape,
        in_specs=[WHOLE] * 2,
        out_specs=WHOLE,
        compiler_params=params(8),
        cost_estimate=cost(8 * rank * rows * LANES, 4 * rows * LANES),
        name="factors",
    )(gram, left)
    new_error, new_momentum, q_next = pl.pallas_call(
        functools.partial(output_kernel, chunks),
        out_shape=out_shapes,
        in_specs=[WHOLE] * 6 + [FAR] * 3,
        out_specs=(FAR,) * 3,
        scratch_shapes=scratch(2),
        input_output_aliases={6: 0, 7: 1, 8: 2},
        compiler_params=params(12),
        name="outputs",
    )(ahead, beside, own, other, base, momentum, *begun)
    return (new_error[None], new_momentum, q_next.T)


def solution(mesh):
    shape = mesh.shape
    fine = Mesh(mesh.devices.reshape(shape["dp"], 4, 8, 2), ("dp", "x", "z", "core"))
    rows = ("x", "z", "core")
    placed = (P("dp", rows, None), P("dp", rows, None), P(rows, None), P())
    return jax.shard_map(
        shards,
        mesh=fine,
        in_specs=placed,
        out_specs=(P("dp", rows, None), P(rows, None), P()),
        check_vma=False,
    )
```

```python
import functools
import jax
import jax.numpy as jnp
from jax import lax
from jax.experimental import pallas as pl
from jax.experimental.pallas import tpu as pltpu
from jax.sharding import Mesh, PartitionSpec as P

HIGHEST = lax.Precision.HIGHEST
F32 = jnp.float32
BF16 = jnp.bfloat16
LANES = 128
TILE = 8
WHOLE = pl.BlockSpec(memory_space=pltpu.VMEM)
FAR = pl.BlockSpec(memory_space=pltpu.HBM)


def split3(value):
    high = value.astype(BF16)
    rest = value - high.astype(F32)
    middle = rest.astype(BF16)
    low = (rest - middle.astype(F32)).astype(BF16)
    return high, middle, low


def nt_dot(first, second, precision=None):
    return lax.dot_general(
        first, second, (((1,), (1,)), ((), ())), precision=precision, preferred_element_type=F32
    )


def left_kernel(parts, grad, error, q_start, term, merged, base, grad_vmem, error_vmem, q_vmem, sems):
    unit = grad.shape[1] // sum(parts)
    slabs = [pl.ds(sum(parts[:step]) * unit, parts[step] * unit) for step in range(len(parts))]
    copies = []
    for step, here in enumerate(slabs):
        group = [
            pltpu.make_async_copy(far.at[:, here], near.at[:, here], sems.at[which, step])
            for which, (far, near) in enumerate(
                ((grad, grad_vmem), (error, error_vmem), (q_start, q_vmem))
            )
        ]
        for copy in group:
            copy.start()
        copies.append(group)
    total = jnp.zeros(term.shape, F32)
    for group, here in zip(copies, slabs):
        for copy in group:
            copy.wait()
        summed = grad_vmem[:, here].astype(F32) + error_vmem[:, here].astype(F32)
        base[:, here] = summed
        low = summed.astype(BF16)
        merged[:, here] = low
        total += nt_dot(q_vmem[:, here].astype(BF16), low)
    term[...] = total


def given_kernel(term, one, two, three, merged, given, gram, left):
    half = merged.shape[1] // 2
    rank = term.shape[0]
    total = (term[...] + two[...]) + (one[...] + three[...])
    left[...] = total
    there = pl.ds(pl.multiple_of((1 - lax.axis_index("core")) * half, LANES), half)
    given[:, :half] = jnp.dot(total.astype(BF16), merged[:, there], preferred_element_type=F32)
    square = nt_dot(total, total, HIGHEST)
    rest = jnp.zeros((TILE, LANES - 2 * rank), F32)
    tile = jnp.concatenate([square[:TILE], square[TILE:], rest], axis=1)
    gram[...] = tile
    given[:TILE, half:] = tile
    given[TILE:, half:] = jnp.zeros((rank - TILE, LANES), F32)


def kept_kernel(left, merged, kept):
    half = merged.shape[1] // 2
    here = pl.ds(pl.multiple_of(lax.axis_index("core") * half, LANES), half)
    kept[...] = jnp.dot(left[...].astype(BF16), merged[:, here], preferred_element_type=F32)


def pieces_kernel(kept, gram, taken, pieces):
    half = kept.shape[1]
    planes, tiles = pieces.shape[:2]
    across = (tiles - 1) // 2
    square = gram[...] + taken[:TILE, half:]
    for index in range(planes):
        for block in range(across):
            here = pl.ds((index * across + block) * LANES, LANES)
            total = kept[:, here] + taken[:, here]
            pieces[index, block] = total[:TILE]
            pieces[index, across + block] = total[TILE:]
        pieces[index, tiles - 1] = square


def plane_kernel(arrived, spread):
    total = arrived[0]
    for index in range(1, arrived.shape[0]):
        total += arrived[index]
    for index in range(spread.shape[0]):
        spread[index] = total


def layer_kernel(groups, arrived, spread, gram):
    tiles = spread.shape[1]
    total = arrived[0]
    for index in range(1, arrived.shape[0]):
        total += arrived[index]
    gram[...] = total[tiles] / groups
    for index in range(spread.shape[0]):
        spread[index] = total[:tiles]


def make_factors(groups, gram, left, factors):
    rank, rows = left.shape
    shape = (rank, LANES)
    row = lax.broadcasted_iota(jnp.int32, shape, 0)
    col = lax.broadcasted_iota(jnp.int32, shape, 1)
    third = (col >= rank) & (col < 2 * rank)
    square = jnp.concatenate([gram[:, :rank], gram[:, rank : 2 * rank]], axis=0)
    rest = jnp.zeros((rank, LANES - 2 * rank - rows), F32)
    table = jnp.concatenate([square, jnp.zeros((rank, rank), F32), left[...], rest], axis=1)
    table = jnp.where(col == row + rank, 1.0, table)
    pivots = jnp.ones(shape, F32)
    for step in range(rank):
        column = jnp.broadcast_to(table[:, step : step + 1], shape)
        scaled = table[step : step + 1, :] / column[step : step + 1, :]
        pivots = jnp.where(row == step, column, pivots)
        change = jnp.where((row < step) & third, 0.0, column * scaled)
        table = jnp.where(row == step, scaled, table - change)
    table = jnp.where(third, table * jnp.sqrt(pivots), table)
    combined = table[:, 2 * rank : 2 * rank + rows].T
    stacked = jnp.concatenate([combined, table[:, rank : 2 * rank]], axis=0) / groups
    high, middle, low = split3(stacked)
    factors[...] = jnp.concatenate([high, high, middle, high, middle, low], axis=1)


def put_halves(chunks, halves, factors, base, momentum, outs, scratch):
    error_vmem, momentum_vmem, q_vmem, sems = scratch
    rows, cols = base.shape
    half = cols // 2
    width = half // chunks
    copies = []
    for turn, (begin, source) in enumerate(halves):
        across = source.shape[1] // 2
        per = width // (across * LANES)
        for chunk in range(chunks):
            parts = []
            for index in range(chunk * per, (chunk + 1) * per):
                for block in range(across):
                    parts.append(jnp.concatenate([source[index, block], source[index, across + block]], axis=0))
            high, middle, low = split3(jnp.concatenate(parts, axis=1))
            depth = jnp.concatenate([high, middle, high, low, middle, high], axis=0)
            product = jnp.dot(factors[...], depth, preferred_element_type=F32)
            approx = product[:rows]
            here = pl.ds(turn * half + chunk * width, width)
            there = pl.ds(begin + chunk * width, width)
            q_vmem[:, here] = product[rows:]
            error_vmem[:, here] = (base[:, there] - approx).astype(BF16)
            momentum_vmem[:, here] = 0.9 * momentum[:, there] + approx
            for which, (near, far) in enumerate(zip((error_vmem, momentum_vmem, q_vmem), outs)):
                copy = pltpu.make_async_copy(
                    near.at[:, here], far.at[:, there], sems.at[which, turn * chunks + chunk]
                )
                copy.start()
                copies.append(copy)
    for copy in copies:
        copy.wait()


def ahead_kernel(groups, chunks, gram, left, own, base, momentum, same, factors, *rest):
    same[...] = own[...]

    @pl.when(lax.axis_index("core") == 1)
    def _():
        make_factors(groups, gram, left, factors)
        half = base.shape[1] // 2
        put_halves(chunks, ((half, own),), factors, base, momentum, rest[:3], rest[3:])


def factor_kernel(groups, gram, left, factors):
    @pl.when(lax.axis_index("core") == 0)
    def _():
        make_factors(groups, gram, left, factors)


def output_kernel(chunks, ahead, beside, own, other, base, momentum, *rest):
    outs, scratch = rest[3:6], rest[6:]
    half = base.shape[1] // 2
    core = lax.axis_index("core")

    @pl.when(core == 0)
    def _():
        put_halves(chunks, ((0, own), (half, other)), beside, base, momentum, outs, scratch)

    @pl.when(core == 1)
    def _():
        put_halves(chunks, ((0, other),), ahead, base, momentum, outs, scratch)


def params(megabytes):
    return pltpu.CompilerParams(vmem_limit_bytes=megabytes * 1024 * 1024)


def cost(flops, moved):
    return pl.CostEstimate(flops=flops, bytes_accessed=moved, transcendentals=0)


def shards(grad, error, momentum, q_start):
    groups = lax.axis_size("dp")
    planes = groups * lax.axis_size("x")
    layers = lax.axis_size("z")
    cols, rank = q_start.shape
    rows = grad.shape[1]
    half = cols // 2
    tiles = rank * half // planes // (TILE * LANES)
    swap = [(0, 1), (1, 0)]
    parts = (1,) * 6

    term, merged, base = pl.pallas_call(
        functools.partial(left_kernel, parts),
        out_shape=(
            pltpu.VMEM((rank, rows), F32),
            pltpu.VMEM((rows, cols), BF16),
            pltpu.VMEM((rows, cols), F32),
        ),
        in_specs=[FAR] * 3,
        out_specs=(WHOLE,) * 3,
        scratch_shapes=[
            pltpu.VMEM((rows, cols), BF16),
            pltpu.VMEM((rows, cols), BF16),
            pltpu.VMEM((rank, cols), F32),
            pltpu.SemaphoreType.DMA((3, len(parts))),
        ],
        compiler_params=params(58),
        name="left_term",
    )(grad[0], error[0], q_start.T)
    two, three, one = (
        lax.ppermute(term, "dp", [(i, (i + k) % groups) for i in range(groups)]) for k in (1, 3, 2)
    )
    one, two = two, one
    given, gram, left = pl.pallas_call(
        given_kernel,
        out_shape=(
            pltpu.VMEM((rank, half + LANES), F32),
            pltpu.VMEM((TILE, LANES), F32),
            pltpu.VMEM((rank, rows), F32),
        ),
        in_specs=[WHOLE] * 5,
        out_specs=(WHOLE,) * 3,
        compiler_params=params(8),
        name="right_given",
    )(term, one, two, three, merged)
    taken = lax.ppermute(given, "core", swap)
    kept = pl.pallas_call(
        kept_kernel,
        out_shape=pltpu.VMEM((rank, half), F32),
        in_specs=[WHOLE] * 2,
        out_specs=WHOLE,
        compiler_params=params(8),
        cost_estimate=cost(2 * rank * rows * half, 4 * rows * half),
        name="right_kept",
    )(left, merged)
    pieces = pl.pallas_call(
        pieces_kernel,
        out_shape=pltpu.VMEM((planes, tiles + 1, TILE, LANES), F32),
        in_specs=[WHOLE] * 3,
        out_specs=WHOLE,
        compiler_params=params(8),
        name="right_pieces",
    )(kept, gram, taken)
    arrived = lax.all_to_all(pieces, ("dp", "x"), 0, 0)
    spread = pl.pallas_call(
        plane_kernel,
        out_shape=pltpu.VMEM((layers, tiles + 1, TILE, LANES), F32),
        in_specs=[WHOLE],
        out_specs=WHOLE,
        compiler_params=params(8),
        name="plane_sum",
    )(arrived)
    arrived = lax.all_to_all(spread, "z", 0, 0)
    spread, gram = pl.pallas_call(
        functools.partial(layer_kernel, groups),
        out_shape=(pltpu.VMEM((planes, tiles, TILE, LANES), F32), pltpu.VMEM((TILE, LANES), F32)),
        in_specs=[WHOLE],
        out_specs=(WHOLE,) * 2,
        compiler_params=params(8),
        name="layer_sum",
    )(arrived)
    own = lax.all_to_all(spread, ("dp", "x"), 0, 0)
    chunks = 4
    shapes = (((rows, cols), BF16), ((rows, cols), F32), ((rank, cols), F32))
    out_shapes = tuple(jax.ShapeDtypeStruct(shape, dtype) for shape, dtype in shapes)
    factor_shape = pltpu.VMEM((rows + rank, 6 * rank), BF16)

    def scratch(halves):
        buffers = [pltpu.VMEM((shape[0], halves * half), dtype) for shape, dtype in shapes]
        return buffers + [pltpu.SemaphoreType.DMA((3, halves * chunks))]

    own, ahead, *begun = pl.pallas_call(
        functools.partial(ahead_kernel, groups, chunks),
        out_shape=(pltpu.VMEM(own.shape, F32), factor_shape) + out_shapes,
        in_specs=[WHOLE] * 5,
        out_specs=(WHOLE,) * 2 + (FAR,) * 3,
        scratch_shapes=scratch(1),
        compiler_params=params(8),
        name="outputs_ahead",
    )(gram, left, own, base, momentum)
    other = lax.ppermute(own, "core", swap)
    beside = pl.pallas_call(
        functools.partial(factor_kernel, groups),
        out_shape=factor_shape,
        in_specs=[WHOLE] * 2,
        out_specs=WHOLE,
        compiler_params=params(8),
        cost_estimate=cost(8 * rank * rows * LANES, 4 * rows * LANES),
        name="factors",
    )(gram, left)
    new_error, new_momentum, q_next = pl.pallas_call(
        functools.partial(output_kernel, chunks),
        out_shape=out_shapes,
        in_specs=[WHOLE] * 6 + [FAR] * 3,
        out_specs=(FAR,) * 3,
        scratch_shapes=scratch(2),
        input_output_aliases={6: 0, 7: 1, 8: 2},
        compiler_params=params(12),
        name="outputs",
    )(ahead, beside, own, other, base, momentum, *begun)
    return (new_error[None], new_momentum, q_next.T)


def solution(mesh):
    shape = mesh.shape
    fine = Mesh(mesh.devices.reshape(shape["dp"], 4, 8, 2), ("dp", "x", "z", "core"))
    rows = ("x", "z", "core")
    placed = (P("dp", rows, None), P("dp", rows, None), P(rows, None), P())
    return jax.shard_map(
        shards,
        mesh=fine,
        in_specs=placed,
        out_specs=(P("dp", rows, None), P(rows, None), P()),
        check_vma=False,
    )
```

```python
import functools
import jax
import jax.numpy as jnp
from jax import lax
from jax.experimental import pallas as pl
from jax.experimental.pallas import tpu as pltpu
from jax.sharding import Mesh, PartitionSpec as P

HIGHEST = lax.Precision.HIGHEST
F32 = jnp.float32
BF16 = jnp.bfloat16
LANES = 128
TILE = 8
WHOLE = pl.BlockSpec(memory_space=pltpu.VMEM)
FAR = pl.BlockSpec(memory_space=pltpu.HBM)


def split3(value):
    high = value.astype(BF16)
    rest = value - high.astype(F32)
    middle = rest.astype(BF16)
    low = (rest - middle.astype(F32)).astype(BF16)
    return high, middle, low


def nt_dot(first, second, precision=None):
    return lax.dot_general(
        first, second, (((1,), (1,)), ((), ())), precision=precision, preferred_element_type=F32
    )


def left_kernel(parts, grad, error, q_start, term, merged, base, grad_vmem, error_vmem, q_vmem, sems):
    unit = grad.shape[1] // sum(parts)
    slabs = [pl.ds(sum(parts[:step]) * unit, parts[step] * unit) for step in range(len(parts))]
    copies = []
    for step, here in enumerate(slabs):
        group = [
            pltpu.make_async_copy(far.at[:, here], near.at[:, here], sems.at[which, step])
            for which, (far, near) in enumerate(
                ((grad, grad_vmem), (error, error_vmem), (q_start, q_vmem))
            )
        ]
        for copy in group:
            copy.start()
        copies.append(group)
    total = jnp.zeros(term.shape, F32)
    for group, here in zip(copies, slabs):
        for copy in group:
            copy.wait()
        summed = grad_vmem[:, here].astype(F32) + error_vmem[:, here].astype(F32)
        base[:, here] = summed
        low = summed.astype(BF16)
        merged[:, here] = low
        total += nt_dot(q_vmem[:, here].astype(BF16), low)
    term[...] = total


def given_kernel(term, three, one, two, merged, given, gram, left):
    half = merged.shape[1] // 2
    rank = term.shape[0]
    total = (term[...] + two[...]) + (one[...] + three[...])
    left[...] = total
    there = pl.ds(pl.multiple_of((1 - lax.axis_index("core")) * half, LANES), half)
    given[:, :half] = jnp.dot(total.astype(BF16), merged[:, there], preferred_element_type=F32)
    square = nt_dot(total, total, HIGHEST)
    rest = jnp.zeros((TILE, LANES - 2 * rank), F32)
    tile = jnp.concatenate([square[:TILE], square[TILE:], rest], axis=1)
    gram[...] = tile
    given[:TILE, half:] = tile
    given[TILE:, half:] = jnp.zeros((rank - TILE, LANES), F32)


def kept_kernel(left, merged, kept):
    half = merged.shape[1] // 2
    here = pl.ds(pl.multiple_of(lax.axis_index("core") * half, LANES), half)
    kept[...] = jnp.dot(left[...].astype(BF16), merged[:, here], preferred_element_type=F32)


def pieces_kernel(kept, gram, taken, pieces):
    half = kept.shape[1]
    planes, tiles = pieces.shape[:2]
    across = (tiles - 1) // 2
    square = gram[...] + taken[:TILE, half:]
    for index in range(planes):
        for block in range(across):
            here = pl.ds((index * across + block) * LANES, LANES)
            total = kept[:, here] + taken[:, here]
            pieces[index, block] = total[:TILE]
            pieces[index, across + block] = total[TILE:]
        pieces[index, tiles - 1] = square


def plane_kernel(arrived, spread):
    total = arrived[0]
    for index in range(1, arrived.shape[0]):
        total += arrived[index]
    for index in range(spread.shape[0]):
        spread[index] = total


def layer_kernel(groups, arrived, spread, gram):
    tiles = spread.shape[1]
    total = arrived[0]
    for index in range(1, arrived.shape[0]):
        total += arrived[index]
    gram[...] = total[tiles] / groups
    for index in range(spread.shape[0]):
        spread[index] = total[:tiles]


def make_factors(groups, gram, left, factors):
    rank, rows = left.shape
    shape = (rank, LANES)
    row = lax.broadcasted_iota(jnp.int32, shape, 0)
    col = lax.broadcasted_iota(jnp.int32, shape, 1)
    third = (col >= rank) & (col < 2 * rank)
    square = jnp.concatenate([gram[:, :rank], gram[:, rank : 2 * rank]], axis=0)
    rest = jnp.zeros((rank, LANES - 2 * rank - rows), F32)
    table = jnp.concatenate([square, jnp.zeros((rank, rank), F32), left[...], rest], axis=1)
    table = jnp.where(col == row + rank, 1.0, table)
    pivots = jnp.ones(shape, F32)
    for step in range(rank):
        column = jnp.broadcast_to(table[:, step : step + 1], shape)
        scaled = table[step : step + 1, :] / column[step : step + 1, :]
        pivots = jnp.where(row == step, column, pivots)
        change = jnp.where((row < step) & third, 0.0, column * scaled)
        table = jnp.where(row == step, scaled, table - change)
    table = jnp.where(third, table * jnp.sqrt(pivots), table)
    combined = table[:, 2 * rank : 2 * rank + rows].T
    stacked = jnp.concatenate([combined, table[:, rank : 2 * rank]], axis=0) / groups
    high, middle, low = split3(stacked)
    factors[...] = jnp.concatenate([high, high, middle, high, middle, low], axis=1)


def put_halves(chunks, halves, factors, base, momentum, outs, scratch):
    error_vmem, momentum_vmem, q_vmem, sems = scratch
    rows, cols = base.shape
    half = cols // 2
    width = half // chunks
    copies = []
    for turn, (begin, source) in enumerate(halves):
        across = source.shape[1] // 2
        per = width // (across * LANES)
        for chunk in range(chunks):
            parts = []
            for index in range(chunk * per, (chunk + 1) * per):
                for block in range(across):
                    parts.append(jnp.concatenate([source[index, block], source[index, across + block]], axis=0))
            high, middle, low = split3(jnp.concatenate(parts, axis=1))
            depth = jnp.concatenate([high, middle, high, low, middle, high], axis=0)
            product = jnp.dot(factors[...], depth, preferred_element_type=F32)
            approx = product[:rows]
            here = pl.ds(turn * half + chunk * width, width)
            there = pl.ds(begin + chunk * width, width)
            q_vmem[:, here] = product[rows:]
            error_vmem[:, here] = (base[:, there] - approx).astype(BF16)
            momentum_vmem[:, here] = 0.9 * momentum[:, there] + approx
            for which, (near, far) in enumerate(zip((error_vmem, momentum_vmem, q_vmem), outs)):
                copy = pltpu.make_async_copy(
                    near.at[:, here], far.at[:, there], sems.at[which, turn * chunks + chunk]
                )
                copy.start()
                copies.append(copy)
    for copy in copies:
        copy.wait()


def ahead_kernel(groups, chunks, gram, left, own, base, momentum, factors, *rest):
    @pl.when(lax.axis_index("core") == 1)
    def _():
        make_factors(groups, gram, left, factors)
        half = base.shape[1] // 2
        put_halves(chunks, ((half, own),), factors, base, momentum, rest[:3], rest[3:])


def factor_kernel(groups, gram, left, factors):
    @pl.when(lax.axis_index("core") == 0)
    def _():
        make_factors(groups, gram, left, factors)


def output_kernel(chunks, ahead, beside, own, other, base, momentum, *rest):
    outs, scratch = rest[3:6], rest[6:]
    half = base.shape[1] // 2
    core = lax.axis_index("core")

    @pl.when(core == 0)
    def _():
        put_halves(chunks, ((0, own), (half, other)), beside, base, momentum, outs, scratch)

    @pl.when(core == 1)
    def _():
        put_halves(chunks, ((0, other),), ahead, base, momentum, outs, scratch)


def params(megabytes):
    return pltpu.CompilerParams(vmem_limit_bytes=megabytes * 1024 * 1024)


def cost(flops, moved):
    return pl.CostEstimate(flops=flops, bytes_accessed=moved, transcendentals=0)


def shards(grad, error, momentum, q_start):
    groups = lax.axis_size("dp")
    planes = groups * lax.axis_size("x")
    layers = lax.axis_size("z")
    cols, rank = q_start.shape
    rows = grad.shape[1]
    half = cols // 2
    tiles = rank * half // planes // (TILE * LANES)
    swap = [(0, 1), (1, 0)]
    parts = (1,) * 6

    term, merged, base = pl.pallas_call(
        functools.partial(left_kernel, parts),
        out_shape=(
            pltpu.VMEM((rank, rows), F32),
            pltpu.VMEM((rows, cols), BF16),
            pltpu.VMEM((rows, cols), F32),
        ),
        in_specs=[FAR] * 3,
        out_specs=(WHOLE,) * 3,
        scratch_shapes=[
            pltpu.VMEM((rows, cols), BF16),
            pltpu.VMEM((rows, cols), BF16),
            pltpu.VMEM((rank, cols), F32),
            pltpu.SemaphoreType.DMA((3, len(parts))),
        ],
        compiler_params=params(58),
        name="left_term",
    )(grad[0], error[0], q_start.T)
    three, one, two = (
        lax.ppermute(term, "dp", [(i, (i + k) % groups) for i in range(groups)]) for k in (3, 1, 2)
    )
    given, gram, left = pl.pallas_call(
        given_kernel,
        out_shape=(
            pltpu.VMEM((rank, half + LANES), F32),
            pltpu.VMEM((TILE, LANES), F32),
            pltpu.VMEM((rank, rows), F32),
        ),
        in_specs=[WHOLE] * 5,
        out_specs=(WHOLE,) * 3,
        compiler_params=params(8),
        name="right_given",
    )(term, three, one, two, merged)
    taken = lax.ppermute(given, "core", swap)
    kept = pl.pallas_call(
        kept_kernel,
        out_shape=pltpu.VMEM((rank, half), F32),
        in_specs=[WHOLE] * 2,
        out_specs=WHOLE,
        compiler_params=params(8),
        cost_estimate=cost(2 * rank * rows * half, 4 * rows * half),
        name="right_kept",
    )(left, merged)
    pieces = pl.pallas_call(
        pieces_kernel,
        out_shape=pltpu.VMEM((planes, tiles + 1, TILE, LANES), F32),
        in_specs=[WHOLE] * 3,
        out_specs=WHOLE,
        compiler_params=params(8),
        name="right_pieces",
    )(kept, gram, taken)
    arrived = lax.all_to_all(pieces, ("dp", "x"), 0, 0)
    spread = pl.pallas_call(
        plane_kernel,
        out_shape=pltpu.VMEM((layers, tiles + 1, TILE, LANES), F32),
        in_specs=[WHOLE],
        out_specs=WHOLE,
        compiler_params=params(8),
        name="plane_sum",
    )(arrived)
    arrived = lax.all_to_all(spread, "z", 0, 0)
    spread, gram = pl.pallas_call(
        functools.partial(layer_kernel, groups),
        out_shape=(pltpu.VMEM((planes, tiles, TILE, LANES), F32), pltpu.VMEM((TILE, LANES), F32)),
        in_specs=[WHOLE],
        out_specs=(WHOLE,) * 2,
        compiler_params=params(8),
        name="layer_sum",
    )(arrived)
    own = lax.all_to_all(spread, ("dp", "x"), 0, 0)
    chunks = 4
    shapes = (((rows, cols), BF16), ((rows, cols), F32), ((rank, cols), F32))
    out_shapes = tuple(jax.ShapeDtypeStruct(shape, dtype) for shape, dtype in shapes)
    factor_shape = pltpu.VMEM((rows + rank, 6 * rank), BF16)

    def scratch(halves):
        buffers = [pltpu.VMEM((shape[0], halves * half), dtype) for shape, dtype in shapes]
        return buffers + [pltpu.SemaphoreType.DMA((3, halves * chunks))]

    ahead, *begun = pl.pallas_call(
        functools.partial(ahead_kernel, groups, chunks),
        out_shape=(factor_shape,) + out_shapes,
        in_specs=[WHOLE] * 5,
        out_specs=(WHOLE,) + (FAR,) * 3,
        scratch_shapes=scratch(1),
        compiler_params=params(8),
        name="outputs_ahead",
    )(gram, left, own, base, momentum)
    own, ahead = lax.optimization_barrier((own, ahead))
    other = lax.ppermute(own, "core", swap)
    beside = pl.pallas_call(
        functools.partial(factor_kernel, groups),
        out_shape=factor_shape,
        in_specs=[WHOLE] * 2,
        out_specs=WHOLE,
        compiler_params=params(8),
        cost_estimate=cost(8 * rank * rows * LANES, 4 * rows * LANES),
        name="factors",
    )(gram, left)
    new_error, new_momentum, q_next = pl.pallas_call(
        functools.partial(output_kernel, chunks),
        out_shape=out_shapes,
        in_specs=[WHOLE] * 6 + [FAR] * 3,
        out_specs=(FAR,) * 3,
        scratch_shapes=scratch(2),
        input_output_aliases={6: 0, 7: 1, 8: 2},
        compiler_params=params(12),
        name="outputs",
    )(ahead, beside, own, other, base, momentum, *begun)
    return (new_error[None], new_momentum, q_next.T)


def solution(mesh):
    shape = mesh.shape
    fine = Mesh(mesh.devices.reshape(shape["dp"], 4, 8, 2), ("dp", "x", "z", "core"))
    rows = ("x", "z", "core")
    placed = (P("dp", rows, None), P("dp", rows, None), P(rows, None), P())
    return jax.shard_map(
        shards,
        mesh=fine,
        in_specs=placed,
        out_specs=(P("dp", rows, None), P(rows, None), P()),
        check_vma=False,
    )
```

```python
import functools
import jax
import jax.numpy as jnp
from jax import lax
from jax.experimental import pallas as pl
from jax.experimental.pallas import tpu as pltpu
from jax.sharding import Mesh, PartitionSpec as P

HIGHEST = lax.Precision.HIGHEST
F32 = jnp.float32
BF16 = jnp.bfloat16
LANES = 128
TILE = 8
WHOLE = pl.BlockSpec(memory_space=pltpu.VMEM)
FAR = pl.BlockSpec(memory_space=pltpu.HBM)


def split3(value):
    high = value.astype(BF16)
    rest = value - high.astype(F32)
    middle = rest.astype(BF16)
    low = (rest - middle.astype(F32)).astype(BF16)
    return high, middle, low


def nt_dot(first, second, precision=None):
    return lax.dot_general(
        first, second, (((1,), (1,)), ((), ())), precision=precision, preferred_element_type=F32
    )


def left_kernel(parts, grad, error, q_start, term, merged, base, grad_vmem, error_vmem, q_vmem, sems):
    unit = grad.shape[1] // sum(parts)
    slabs = [pl.ds(sum(parts[:step]) * unit, parts[step] * unit) for step in range(len(parts))]
    copies = []
    for step, here in enumerate(slabs):
        group = [
            pltpu.make_async_copy(far.at[:, here], near.at[:, here], sems.at[which, step])
            for which, (far, near) in enumerate(
                ((grad, grad_vmem), (error, error_vmem), (q_start, q_vmem))
            )
        ]
        for copy in group:
            copy.start()
        copies.append(group)
    total = jnp.zeros(term.shape, F32)
    for group, here in zip(copies, slabs):
        for copy in group:
            copy.wait()
        summed = grad_vmem[:, here].astype(F32) + error_vmem[:, here].astype(F32)
        base[:, here] = summed
        low = summed.astype(BF16)
        merged[:, here] = low
        total += nt_dot(q_vmem[:, here].astype(BF16), low)
    term[...] = total


def given_kernel(term, one, two, three, merged, given, gram, left):
    half = merged.shape[1] // 2
    rank = term.shape[0]
    total = (term[...] + two[...]) + (one[...] + three[...])
    left[...] = total
    there = pl.ds(pl.multiple_of((1 - lax.axis_index("core")) * half, LANES), half)
    given[:, :half] = jnp.dot(total.astype(BF16), merged[:, there], preferred_element_type=F32)
    square = nt_dot(total, total, HIGHEST)
    rest = jnp.zeros((TILE, LANES - 2 * rank), F32)
    tile = jnp.concatenate([square[:TILE], square[TILE:], rest], axis=1)
    gram[...] = tile
    given[:TILE, half:] = tile
    given[TILE:, half:] = jnp.zeros((rank - TILE, LANES), F32)


def kept_kernel(left, merged, kept):
    half = merged.shape[1] // 2
    here = pl.ds(pl.multiple_of(lax.axis_index("core") * half, LANES), half)
    kept[...] = jnp.dot(left[...].astype(BF16), merged[:, here], preferred_element_type=F32)


def pieces_kernel(kept, gram, taken, pieces):
    half = kept.shape[1]
    planes, tiles = pieces.shape[:2]
    across = (tiles - 1) // 2
    square = gram[...] + taken[:TILE, half:]
    for index in range(planes):
        for block in range(across):
            here = pl.ds((index * across + block) * LANES, LANES)
            total = kept[:, here] + taken[:, here]
            pieces[index, block] = total[:TILE]
            pieces[index, across + block] = total[TILE:]
        pieces[index, tiles - 1] = square


def plane_kernel(arrived, spread):
    total = arrived[0]
    for index in range(1, arrived.shape[0]):
        total += arrived[index]
    for index in range(spread.shape[0]):
        spread[index] = total


def layer_kernel(groups, arrived, spread, gram):
    tiles = spread.shape[1]
    total = arrived[0]
    for index in range(1, arrived.shape[0]):
        total += arrived[index]
    gram[...] = total[tiles] / groups
    for index in range(spread.shape[0]):
        spread[index] = total[:tiles]


def make_factors(groups, gram, left, factors):
    rank, rows = left.shape
    shape = (rank, LANES)
    row = lax.broadcasted_iota(jnp.int32, shape, 0)
    col = lax.broadcasted_iota(jnp.int32, shape, 1)
    third = (col >= rank) & (col < 2 * rank)
    square = jnp.concatenate([gram[:, :rank], gram[:, rank : 2 * rank]], axis=0)
    rest = jnp.zeros((rank, LANES - 2 * rank - rows), F32)
    table = jnp.concatenate([square, jnp.zeros((rank, rank), F32), left[...], rest], axis=1)
    table = jnp.where(col == row + rank, 1.0, table)
    pivots = jnp.ones(shape, F32)
    for step in range(rank):
        column = jnp.broadcast_to(table[:, step : step + 1], shape)
        scaled = table[step : step + 1, :] / column[step : step + 1, :]
        pivots = jnp.where(row == step, column, pivots)
        change = jnp.where((row < step) & third, 0.0, column * scaled)
        table = jnp.where(row == step, scaled, table - change)
    table = jnp.where(third, table * jnp.sqrt(pivots), table)
    combined = table[:, 2 * rank : 2 * rank + rows].T
    stacked = jnp.concatenate([combined, table[:, rank : 2 * rank]], axis=0) / groups
    high, middle, low = split3(stacked)
    factors[...] = jnp.concatenate([high, high, middle, high, middle, low], axis=1)


def put_halves(chunks, halves, factors, base, momentum, outs, scratch):
    error_vmem, momentum_vmem, q_vmem, sems = scratch
    rows, cols = base.shape
    half = cols // 2
    width = half // chunks
    copies = []
    for turn, (begin, source) in enumerate(halves):
        across = source.shape[1] // 2
        per = width // (across * LANES)
        for chunk in range(chunks):
            parts = []
            for index in range(chunk * per, (chunk + 1) * per):
                for block in range(across):
                    parts.append(jnp.concatenate([source[index, block], source[index, across + block]], axis=0))
            high, middle, low = split3(jnp.concatenate(parts, axis=1))
            depth = jnp.concatenate([high, middle, high, low, middle, high], axis=0)
            product = jnp.dot(factors[...], depth, preferred_element_type=F32)
            approx = product[:rows]
            here = pl.ds(turn * half + chunk * width, width)
            there = pl.ds(begin + chunk * width, width)
            q_vmem[:, here] = product[rows:]
            error_vmem[:, here] = (base[:, there] - approx).astype(BF16)
            momentum_vmem[:, here] = 0.9 * momentum[:, there] + approx
            for which, (near, far) in enumerate(zip((error_vmem, momentum_vmem, q_vmem), outs)):
                copy = pltpu.make_async_copy(
                    near.at[:, here], far.at[:, there], sems.at[which, turn * chunks + chunk]
                )
                copy.start()
                copies.append(copy)
    for copy in copies:
        copy.wait()


def ahead_kernel(groups, chunks, gram, left, own, base, momentum, factors, *rest):
    @pl.when(lax.axis_index("core") == 1)
    def _():
        make_factors(groups, gram, left, factors)
        half = base.shape[1] // 2
        put_halves(chunks, ((half, own),), factors, base, momentum, rest[:3], rest[3:])


def factor_kernel(groups, gram, left, factors):
    @pl.when(lax.axis_index("core") == 0)
    def _():
        make_factors(groups, gram, left, factors)


def output_kernel(chunks, ahead, beside, own, other, base, momentum, *rest):
    outs, scratch = rest[3:6], rest[6:]
    half = base.shape[1] // 2
    core = lax.axis_index("core")

    @pl.when(core == 0)
    def _():
        put_halves(chunks, ((0, own), (half, other)), beside, base, momentum, outs, scratch)

    @pl.when(core == 1)
    def _():
        put_halves(chunks, ((0, other),), ahead, base, momentum, outs, scratch)


def params(megabytes):
    return pltpu.CompilerParams(vmem_limit_bytes=megabytes * 1024 * 1024)


def cost(flops, moved):
    return pl.CostEstimate(flops=flops, bytes_accessed=moved, transcendentals=0)


def shards(grad, error, momentum, q_start):
    groups = lax.axis_size("dp")
    planes = groups * lax.axis_size("x")
    layers = lax.axis_size("z")
    cols, rank = q_start.shape
    rows = grad.shape[1]
    half = cols // 2
    tiles = rank * half // planes // (TILE * LANES)
    swap = [(0, 1), (1, 0)]
    parts = (1,) * 6

    term, merged, base = pl.pallas_call(
        functools.partial(left_kernel, parts),
        out_shape=(
            pltpu.VMEM((rank, rows), F32),
            pltpu.VMEM((rows, cols), BF16),
            pltpu.VMEM((rows, cols), F32),
        ),
        in_specs=[FAR] * 3,
        out_specs=(WHOLE,) * 3,
        scratch_shapes=[
            pltpu.VMEM((rows, cols), BF16),
            pltpu.VMEM((rows, cols), BF16),
            pltpu.VMEM((rank, cols), F32),
            pltpu.SemaphoreType.DMA((3, len(parts))),
        ],
        compiler_params=params(58),
        name="left_term",
    )(grad[0], error[0], q_start.T)
    one, two, three = (
        lax.ppermute(term, "dp", [(i, (i + k) % groups) for i in range(groups)]) for k in (1, 2, 3)
    )
    given, gram, left = pl.pallas_call(
        given_kernel,
        out_shape=(
            pltpu.VMEM((rank, half + LANES), F32),
            pltpu.VMEM((TILE, LANES), F32),
            pltpu.VMEM((rank, rows), F32),
        ),
        in_specs=[WHOLE] * 5,
        out_specs=(WHOLE,) * 3,
        compiler_params=params(8),
        name="right_given",
    )(term, one, two, three, merged)
    taken = lax.ppermute(given, "core", swap)
    kept = pl.pallas_call(
        kept_kernel,
        out_shape=pltpu.VMEM((rank, half), F32),
        in_specs=[WHOLE] * 2,
        out_specs=WHOLE,
        compiler_params=params(8),
        cost_estimate=cost(2 * rank * rows * half, 4 * rows * half),
        name="right_kept",
    )(left, merged)
    pieces = pl.pallas_call(
        pieces_kernel,
        out_shape=pltpu.VMEM((planes, tiles + 1, TILE, LANES), F32),
        in_specs=[WHOLE] * 3,
        out_specs=WHOLE,
        compiler_params=params(8),
        name="right_pieces",
    )(kept, gram, taken)
    arrived = lax.all_to_all(pieces, ("dp", "x"), 0, 0)
    spread = pl.pallas_call(
        plane_kernel,
        out_shape=pltpu.VMEM((layers, tiles + 1, TILE, LANES), F32),
        in_specs=[WHOLE],
        out_specs=WHOLE,
        compiler_params=params(8),
        name="plane_sum",
    )(arrived)
    arrived = lax.all_to_all(spread, "z", 0, 0)
    spread, gram = pl.pallas_call(
        functools.partial(layer_kernel, groups),
        out_shape=(pltpu.VMEM((planes, tiles, TILE, LANES), F32), pltpu.VMEM((TILE, LANES), F32)),
        in_specs=[WHOLE],
        out_specs=(WHOLE,) * 2,
        compiler_params=params(8),
        name="layer_sum",
    )(arrived)
    own = lax.all_to_all(spread, ("dp", "x"), 0, 0)
    chunks = 4
    shapes = (((rows, cols), BF16), ((rows, cols), F32), ((rank, cols), F32))
    out_shapes = tuple(jax.ShapeDtypeStruct(shape, dtype) for shape, dtype in shapes)
    factor_shape = pltpu.VMEM((rows + rank, 6 * rank), BF16)

    def scratch(halves):
        buffers = [pltpu.VMEM((shape[0], halves * half), dtype) for shape, dtype in shapes]
        return buffers + [pltpu.SemaphoreType.DMA((3, halves * chunks))]

    ahead, *begun = pl.pallas_call(
        functools.partial(ahead_kernel, groups, chunks),
        out_shape=(factor_shape,) + out_shapes,
        in_specs=[WHOLE] * 5,
        out_specs=(WHOLE,) + (FAR,) * 3,
        scratch_shapes=scratch(1),
        compiler_params=params(8),
        name="outputs_ahead",
    )(gram, left, own, base, momentum)
    own, ahead = lax.optimization_barrier((own, ahead))
    other = lax.ppermute(own, "core", swap)
    beside = pl.pallas_call(
        functools.partial(factor_kernel, groups),
        out_shape=factor_shape,
        in_specs=[WHOLE] * 2,
        out_specs=WHOLE,
        compiler_params=params(8),
        cost_estimate=cost(8 * rank * rows * LANES, 4 * rows * LANES),
        name="factors",
    )(gram, left)
    new_error, new_momentum, q_next = pl.pallas_call(
        functools.partial(output_kernel, chunks),
        out_shape=out_shapes,
        in_specs=[WHOLE] * 6 + [FAR] * 3,
        out_specs=(FAR,) * 3,
        scratch_shapes=scratch(2),
        input_output_aliases={6: 0, 7: 1, 8: 2},
        compiler_params=params(12),
        name="outputs",
    )(ahead, beside, own, other, base, momentum, *begun)
    return (new_error[None], new_momentum, q_next.T)


def solution(mesh):
    shape = mesh.shape
    fine = Mesh(mesh.devices.reshape(shape["dp"], 4, 8, 2), ("dp", "x", "z", "core"))
    rows = ("x", "z", "core")
    placed = (P("dp", rows, None), P("dp", rows, None), P(rows, None), P())
    return jax.shard_map(
        shards,
        mesh=fine,
        in_specs=placed,
        out_specs=(P("dp", rows, None), P(rows, None), P()),
        check_vma=False,
    )
```

```python
import functools
import jax
import jax.numpy as jnp
from jax import lax
from jax.experimental import pallas as pl
from jax.experimental.pallas import tpu as pltpu
from jax.sharding import Mesh, PartitionSpec as P

HIGHEST = lax.Precision.HIGHEST
F32 = jnp.float32
BF16 = jnp.bfloat16
LANES = 128
TILE = 8
WHOLE = pl.BlockSpec(memory_space=pltpu.VMEM)
FAR = pl.BlockSpec(memory_space=pltpu.HBM)


def split3(value):
    high = value.astype(BF16)
    rest = value - high.astype(F32)
    middle = rest.astype(BF16)
    low = (rest - middle.astype(F32)).astype(BF16)
    return high, middle, low


def nt_dot(first, second, precision=None):
    return lax.dot_general(
        first, second, (((1,), (1,)), ((), ())), precision=precision, preferred_element_type=F32
    )


def left_kernel(parts, grad, error, q_start, term, merged, base, grad_vmem, error_vmem, q_vmem, sems):
    unit = grad.shape[1] // sum(parts)
    slabs = [pl.ds(sum(parts[:step]) * unit, parts[step] * unit) for step in range(len(parts))]
    copies = []
    for step, here in enumerate(slabs):
        group = [
            pltpu.make_async_copy(far.at[:, here], near.at[:, here], sems.at[which, step])
            for which, (far, near) in enumerate(
                ((grad, grad_vmem), (error, error_vmem), (q_start, q_vmem))
            )
        ]
        for copy in group:
            copy.start()
        copies.append(group)
    total = jnp.zeros(term.shape, F32)
    for group, here in zip(copies, slabs):
        for copy in group:
            copy.wait()
        summed = grad_vmem[:, here].astype(F32) + error_vmem[:, here].astype(F32)
        base[:, here] = summed
        low = summed.astype(BF16)
        merged[:, here] = low
        total += nt_dot(q_vmem[:, here].astype(BF16), low)
    term[...] = total


def given_kernel(term, two, one, three, merged, given, gram, left):
    half = merged.shape[1] // 2
    rank = term.shape[0]
    total = (term[...] + two[...]) + (one[...] + three[...])
    left[...] = total
    there = pl.ds(pl.multiple_of((1 - lax.axis_index("core")) * half, LANES), half)
    given[:, :half] = jnp.dot(total.astype(BF16), merged[:, there], preferred_element_type=F32)
    square = nt_dot(total, total, HIGHEST)
    rest = jnp.zeros((TILE, LANES - 2 * rank), F32)
    tile = jnp.concatenate([square[:TILE], square[TILE:], rest], axis=1)
    gram[...] = tile
    given[:TILE, half:] = tile
    given[TILE:, half:] = jnp.zeros((rank - TILE, LANES), F32)


def kept_kernel(left, merged, kept):
    half = merged.shape[1] // 2
    here = pl.ds(pl.multiple_of(lax.axis_index("core") * half, LANES), half)
    kept[...] = jnp.dot(left[...].astype(BF16), merged[:, here], preferred_element_type=F32)


def pieces_kernel(kept, gram, taken, pieces):
    half = kept.shape[1]
    planes, tiles = pieces.shape[:2]
    across = (tiles - 1) // 2
    square = gram[...] + taken[:TILE, half:]
    for index in range(planes):
        for block in range(across):
            here = pl.ds((index * across + block) * LANES, LANES)
            total = kept[:, here] + taken[:, here]
            pieces[index, block] = total[:TILE]
            pieces[index, across + block] = total[TILE:]
        pieces[index, tiles - 1] = square


def plane_kernel(arrived, spread):
    total = arrived[0]
    for index in range(1, arrived.shape[0]):
        total += arrived[index]
    for index in range(spread.shape[0]):
        spread[index] = total


def layer_kernel(groups, arrived, spread, gram):
    tiles = spread.shape[1]
    total = arrived[0]
    for index in range(1, arrived.shape[0]):
        total += arrived[index]
    gram[...] = total[tiles] / groups
    for index in range(spread.shape[0]):
        spread[index] = total[:tiles]


def make_factors(groups, gram, left, factors):
    rank, rows = left.shape
    shape = (rank, LANES)
    row = lax.broadcasted_iota(jnp.int32, shape, 0)
    col = lax.broadcasted_iota(jnp.int32, shape, 1)
    third = (col >= rank) & (col < 2 * rank)
    square = jnp.concatenate([gram[:, :rank], gram[:, rank : 2 * rank]], axis=0)
    rest = jnp.zeros((rank, LANES - 2 * rank - rows), F32)
    table = jnp.concatenate([square, jnp.zeros((rank, rank), F32), left[...], rest], axis=1)
    table = jnp.where(col == row + rank, 1.0, table)
    pivots = jnp.ones(shape, F32)
    for step in range(rank):
        column = jnp.broadcast_to(table[:, step : step + 1], shape)
        scaled = table[step : step + 1, :] / column[step : step + 1, :]
        pivots = jnp.where(row == step, column, pivots)
        change = jnp.where((row < step) & third, 0.0, column * scaled)
        table = jnp.where(row == step, scaled, table - change)
    table = jnp.where(third, table * jnp.sqrt(pivots), table)
    combined = table[:, 2 * rank : 2 * rank + rows].T
    stacked = jnp.concatenate([combined, table[:, rank : 2 * rank]], axis=0) / groups
    high, middle, low = split3(stacked)
    factors[...] = jnp.concatenate([high, high, middle, high, middle, low], axis=1)


def put_halves(chunks, halves, factors, base, momentum, outs, scratch):
    error_vmem, momentum_vmem, q_vmem, sems = scratch
    rows, cols = base.shape
    half = cols // 2
    width = half // chunks
    copies = []
    for turn, (begin, source) in enumerate(halves):
        across = source.shape[1] // 2
        per = width // (across * LANES)
        for chunk in range(chunks):
            parts = []
            for index in range(chunk * per, (chunk + 1) * per):
                for block in range(across):
                    parts.append(jnp.concatenate([source[index, block], source[index, across + block]], axis=0))
            high, middle, low = split3(jnp.concatenate(parts, axis=1))
            depth = jnp.concatenate([high, middle, high, low, middle, high], axis=0)
            product = jnp.dot(factors[...], depth, preferred_element_type=F32)
            approx = product[:rows]
            here = pl.ds(turn * half + chunk * width, width)
            there = pl.ds(begin + chunk * width, width)
            q_vmem[:, here] = product[rows:]
            error_vmem[:, here] = (base[:, there] - approx).astype(BF16)
            momentum_vmem[:, here] = 0.9 * momentum[:, there] + approx
            for which, (near, far) in enumerate(zip((error_vmem, momentum_vmem, q_vmem), outs)):
                copy = pltpu.make_async_copy(
                    near.at[:, here], far.at[:, there], sems.at[which, turn * chunks + chunk]
                )
                copy.start()
                copies.append(copy)
    for copy in copies:
        copy.wait()


def ahead_kernel(groups, chunks, gram, left, own, base, momentum, factors, *rest):
    @pl.when(lax.axis_index("core") == 1)
    def _():
        make_factors(groups, gram, left, factors)
        half = base.shape[1] // 2
        put_halves(chunks, ((half, own),), factors, base, momentum, rest[:3], rest[3:])


def factor_kernel(groups, gram, left, factors):
    @pl.when(lax.axis_index("core") == 0)
    def _():
        make_factors(groups, gram, left, factors)


def output_kernel(chunks, ahead, beside, own, other, base, momentum, *rest):
    outs, scratch = rest[3:6], rest[6:]
    half = base.shape[1] // 2
    core = lax.axis_index("core")

    @pl.when(core == 0)
    def _():
        put_halves(chunks, ((0, own), (half, other)), beside, base, momentum, outs, scratch)

    @pl.when(core == 1)
    def _():
        put_halves(chunks, ((0, other),), ahead, base, momentum, outs, scratch)


def params(megabytes):
    return pltpu.CompilerParams(vmem_limit_bytes=megabytes * 1024 * 1024)


def cost(flops, moved):
    return pl.CostEstimate(flops=flops, bytes_accessed=moved, transcendentals=0)


def shards(grad, error, momentum, q_start):
    groups = lax.axis_size("dp")
    planes = groups * lax.axis_size("x")
    layers = lax.axis_size("z")
    cols, rank = q_start.shape
    rows = grad.shape[1]
    half = cols // 2
    tiles = rank * half // planes // (TILE * LANES)
    swap = [(0, 1), (1, 0)]
    parts = (1,) * 6

    term, merged, base = pl.pallas_call(
        functools.partial(left_kernel, parts),
        out_shape=(
            pltpu.VMEM((rank, rows), F32),
            pltpu.VMEM((rows, cols), BF16),
            pltpu.VMEM((rows, cols), F32),
        ),
        in_specs=[FAR] * 3,
        out_specs=(WHOLE,) * 3,
        scratch_shapes=[
            pltpu.VMEM((rows, cols), BF16),
            pltpu.VMEM((rows, cols), BF16),
            pltpu.VMEM((rank, cols), F32),
            pltpu.SemaphoreType.DMA((3, len(parts))),
        ],
        compiler_params=params(58),
        name="left_term",
    )(grad[0], error[0], q_start.T)
    two, one, three = (
        lax.ppermute(term, "dp", [(i, (i + k) % groups) for i in range(groups)]) for k in (2, 1, 3)
    )
    given, gram, left = pl.pallas_call(
        given_kernel,
        out_shape=(
            pltpu.VMEM((rank, half + LANES), F32),
            pltpu.VMEM((TILE, LANES), F32),
            pltpu.VMEM((rank, rows), F32),
        ),
        in_specs=[WHOLE] * 5,
        out_specs=(WHOLE,) * 3,
        compiler_params=params(8),
        name="right_given",
    )(term, two, one, three, merged)
    taken = lax.ppermute(given, "core", swap)
    kept = pl.pallas_call(
        kept_kernel,
        out_shape=pltpu.VMEM((rank, half), F32),
        in_specs=[WHOLE] * 2,
        out_specs=WHOLE,
        compiler_params=params(8),
        cost_estimate=cost(2 * rank * rows * half, 4 * rows * half),
        name="right_kept",
    )(left, merged)
    pieces = pl.pallas_call(
        pieces_kernel,
        out_shape=pltpu.VMEM((planes, tiles + 1, TILE, LANES), F32),
        in_specs=[WHOLE] * 3,
        out_specs=WHOLE,
        compiler_params=params(8),
        name="right_pieces",
    )(kept, gram, taken)
    arrived = lax.all_to_all(pieces, ("dp", "x"), 0, 0)
    spread = pl.pallas_call(
        plane_kernel,
        out_shape=pltpu.VMEM((layers, tiles + 1, TILE, LANES), F32),
        in_specs=[WHOLE],
        out_specs=WHOLE,
        compiler_params=params(8),
        name="plane_sum",
    )(arrived)
    arrived = lax.all_to_all(spread, "z", 0, 0)
    spread, gram = pl.pallas_call(
        functools.partial(layer_kernel, groups),
        out_shape=(pltpu.VMEM((planes, tiles, TILE, LANES), F32), pltpu.VMEM((TILE, LANES), F32)),
        in_specs=[WHOLE],
        out_specs=(WHOLE,) * 2,
        compiler_params=params(8),
        name="layer_sum",
    )(arrived)
    own = lax.all_to_all(spread, ("dp", "x"), 0, 0)
    chunks = 4
    shapes = (((rows, cols), BF16), ((rows, cols), F32), ((rank, cols), F32))
    out_shapes = tuple(jax.ShapeDtypeStruct(shape, dtype) for shape, dtype in shapes)
    factor_shape = pltpu.VMEM((rows + rank, 6 * rank), BF16)

    def scratch(halves):
        buffers = [pltpu.VMEM((shape[0], halves * half), dtype) for shape, dtype in shapes]
        return buffers + [pltpu.SemaphoreType.DMA((3, halves * chunks))]

    ahead, *begun = pl.pallas_call(
        functools.partial(ahead_kernel, groups, chunks),
        out_shape=(factor_shape,) + out_shapes,
        in_specs=[WHOLE] * 5,
        out_specs=(WHOLE,) + (FAR,) * 3,
        scratch_shapes=scratch(1),
        compiler_params=params(8),
        name="outputs_ahead",
    )(gram, left, own, base, momentum)
    own, ahead = lax.optimization_barrier((own, ahead))
    other = lax.ppermute(own, "core", swap)
    beside = pl.pallas_call(
        functools.partial(factor_kernel, groups),
        out_shape=factor_shape,
        in_specs=[WHOLE] * 2,
        out_specs=WHOLE,
        compiler_params=params(8),
        cost_estimate=cost(8 * rank * rows * LANES, 4 * rows * LANES),
        name="factors",
    )(gram, left)
    new_error, new_momentum, q_next = pl.pallas_call(
        functools.partial(output_kernel, chunks),
        out_shape=out_shapes,
        in_specs=[WHOLE] * 6 + [FAR] * 3,
        out_specs=(FAR,) * 3,
        scratch_shapes=scratch(2),
        input_output_aliases={6: 0, 7: 1, 8: 2},
        compiler_params=params(12),
        name="outputs",
    )(ahead, beside, own, other, base, momentum, *begun)
    return (new_error[None], new_momentum, q_next.T)


def solution(mesh):
    shape = mesh.shape
    fine = Mesh(mesh.devices.reshape(shape["dp"], 4, 8, 2), ("dp", "x", "z", "core"))
    rows = ("x", "z", "core")
    placed = (P("dp", rows, None), P("dp", rows, None), P(rows, None), P())
    return jax.shard_map(
        shards,
        mesh=fine,
        in_specs=placed,
        out_specs=(P("dp", rows, None), P(rows, None), P()),
        check_vma=False,
    )
```

```python
import functools
import jax
import jax.numpy as jnp
from jax import lax
from jax.experimental import pallas as pl
from jax.experimental.pallas import tpu as pltpu
from jax.sharding import Mesh, PartitionSpec as P

HIGHEST = lax.Precision.HIGHEST
F32 = jnp.float32
BF16 = jnp.bfloat16
LANES = 128
TILE = 8
WHOLE = pl.BlockSpec(memory_space=pltpu.VMEM)
FAR = pl.BlockSpec(memory_space=pltpu.HBM)


def split3(value):
    high = value.astype(BF16)
    rest = value - high.astype(F32)
    middle = rest.astype(BF16)
    low = (rest - middle.astype(F32)).astype(BF16)
    return high, middle, low


def nt_dot(first, second, precision=None):
    return lax.dot_general(
        first, second, (((1,), (1,)), ((), ())), precision=precision, preferred_element_type=F32
    )


def left_kernel(parts, grad, error, q_start, term, merged, base, grad_vmem, error_vmem, q_vmem, sems):
    unit = grad.shape[1] // sum(parts)
    slabs = [pl.ds(sum(parts[:step]) * unit, parts[step] * unit) for step in range(len(parts))]
    copies = []
    for step, here in enumerate(slabs):
        group = [
            pltpu.make_async_copy(far.at[:, here], near.at[:, here], sems.at[which, step])
            for which, (far, near) in enumerate(
                ((grad, grad_vmem), (error, error_vmem), (q_start, q_vmem))
            )
        ]
        for copy in group:
            copy.start()
        copies.append(group)
    total = jnp.zeros(term.shape, F32)
    for group, here in zip(copies, slabs):
        for copy in group:
            copy.wait()
        summed = grad_vmem[:, here].astype(F32) + error_vmem[:, here].astype(F32)
        base[:, here] = summed
        low = summed.astype(BF16)
        merged[:, here] = low
        total += nt_dot(q_vmem[:, here].astype(BF16), low)
    term[...] = total


def given_kernel(term, one, three, two, merged, given, gram, left):
    half = merged.shape[1] // 2
    rank = term.shape[0]
    total = (term[...] + two[...]) + (one[...] + three[...])
    left[...] = total
    there = pl.ds(pl.multiple_of((1 - lax.axis_index("core")) * half, LANES), half)
    given[:, :half] = jnp.dot(total.astype(BF16), merged[:, there], preferred_element_type=F32)
    square = nt_dot(total, total, HIGHEST)
    rest = jnp.zeros((TILE, LANES - 2 * rank), F32)
    tile = jnp.concatenate([square[:TILE], square[TILE:], rest], axis=1)
    gram[...] = tile
    given[:TILE, half:] = tile
    given[TILE:, half:] = jnp.zeros((rank - TILE, LANES), F32)


def kept_kernel(left, merged, kept):
    half = merged.shape[1] // 2
    here = pl.ds(pl.multiple_of(lax.axis_index("core") * half, LANES), half)
    kept[...] = jnp.dot(left[...].astype(BF16), merged[:, here], preferred_element_type=F32)


def pieces_kernel(kept, gram, taken, pieces):
    half = kept.shape[1]
    planes, tiles = pieces.shape[:2]
    across = (tiles - 1) // 2
    square = gram[...] + taken[:TILE, half:]
    for index in range(planes):
        for block in range(across):
            here = pl.ds((index * across + block) * LANES, LANES)
            total = kept[:, here] + taken[:, here]
            pieces[index, block] = total[:TILE]
            pieces[index, across + block] = total[TILE:]
        pieces[index, tiles - 1] = square


def plane_kernel(arrived, spread):
    total = arrived[0]
    for index in range(1, arrived.shape[0]):
        total += arrived[index]
    for index in range(spread.shape[0]):
        spread[index] = total


def layer_kernel(groups, arrived, spread, gram):
    tiles = spread.shape[1]
    total = arrived[0]
    for index in range(1, arrived.shape[0]):
        total += arrived[index]
    gram[...] = total[tiles] / groups
    for index in range(spread.shape[0]):
        spread[index] = total[:tiles]


def make_factors(groups, gram, left, factors):
    rank, rows = left.shape
    shape = (rank, LANES)
    row = lax.broadcasted_iota(jnp.int32, shape, 0)
    col = lax.broadcasted_iota(jnp.int32, shape, 1)
    third = (col >= rank) & (col < 2 * rank)
    square = jnp.concatenate([gram[:, :rank], gram[:, rank : 2 * rank]], axis=0)
    rest = jnp.zeros((rank, LANES - 2 * rank - rows), F32)
    table = jnp.concatenate([square, jnp.zeros((rank, rank), F32), left[...], rest], axis=1)
    table = jnp.where(col == row + rank, 1.0, table)
    pivots = jnp.ones(shape, F32)
    for step in range(rank):
        column = jnp.broadcast_to(table[:, step : step + 1], shape)
        scaled = table[step : step + 1, :] / column[step : step + 1, :]
        pivots = jnp.where(row == step, column, pivots)
        change = jnp.where((row < step) & third, 0.0, column * scaled)
        table = jnp.where(row == step, scaled, table - change)
    table = jnp.where(third, table * jnp.sqrt(pivots), table)
    combined = table[:, 2 * rank : 2 * rank + rows].T
    stacked = jnp.concatenate([combined, table[:, rank : 2 * rank]], axis=0) / groups
    high, middle, low = split3(stacked)
    factors[...] = jnp.concatenate([high, high, middle, high, middle, low], axis=1)


def put_halves(chunks, halves, factors, base, momentum, outs, scratch):
    error_vmem, momentum_vmem, q_vmem, sems = scratch
    rows, cols = base.shape
    half = cols // 2
    width = half // chunks
    copies = []
    for turn, (begin, source) in enumerate(halves):
        across = source.shape[1] // 2
        per = width // (across * LANES)
        for chunk in range(chunks):
            parts = []
            for index in range(chunk * per, (chunk + 1) * per):
                for block in range(across):
                    parts.append(jnp.concatenate([source[index, block], source[index, across + block]], axis=0))
            high, middle, low = split3(jnp.concatenate(parts, axis=1))
            depth = jnp.concatenate([high, middle, high, low, middle, high], axis=0)
            product = jnp.dot(factors[...], depth, preferred_element_type=F32)
            approx = product[:rows]
            here = pl.ds(turn * half + chunk * width, width)
            there = pl.ds(begin + chunk * width, width)
            q_vmem[:, here] = product[rows:]
            error_vmem[:, here] = (base[:, there] - approx).astype(BF16)
            momentum_vmem[:, here] = 0.9 * momentum[:, there] + approx
            for which, (near, far) in enumerate(zip((error_vmem, momentum_vmem, q_vmem), outs)):
                copy = pltpu.make_async_copy(
                    near.at[:, here], far.at[:, there], sems.at[which, turn * chunks + chunk]
                )
                copy.start()
                copies.append(copy)
    for copy in copies:
        copy.wait()


def ahead_kernel(groups, chunks, gram, left, own, base, momentum, factors, *rest):
    @pl.when(lax.axis_index("core") == 1)
    def _():
        make_factors(groups, gram, left, factors)
        half = base.shape[1] // 2
        put_halves(chunks, ((half, own),), factors, base, momentum, rest[:3], rest[3:])


def factor_kernel(groups, gram, left, factors):
    @pl.when(lax.axis_index("core") == 0)
    def _():
        make_factors(groups, gram, left, factors)


def output_kernel(chunks, ahead, beside, own, other, base, momentum, *rest):
    outs, scratch = rest[3:6], rest[6:]
    half = base.shape[1] // 2
    core = lax.axis_index("core")

    @pl.when(core == 0)
    def _():
        put_halves(chunks, ((0, own), (half, other)), beside, base, momentum, outs, scratch)

    @pl.when(core == 1)
    def _():
        put_halves(chunks, ((0, other),), ahead, base, momentum, outs, scratch)


def params(megabytes):
    return pltpu.CompilerParams(vmem_limit_bytes=megabytes * 1024 * 1024)


def cost(flops, moved):
    return pl.CostEstimate(flops=flops, bytes_accessed=moved, transcendentals=0)


def shards(grad, error, momentum, q_start):
    groups = lax.axis_size("dp")
    planes = groups * lax.axis_size("x")
    layers = lax.axis_size("z")
    cols, rank = q_start.shape
    rows = grad.shape[1]
    half = cols // 2
    tiles = rank * half // planes // (TILE * LANES)
    swap = [(0, 1), (1, 0)]
    parts = (1,) * 6

    term, merged, base = pl.pallas_call(
        functools.partial(left_kernel, parts),
        out_shape=(
            pltpu.VMEM((rank, rows), F32),
            pltpu.VMEM((rows, cols), BF16),
            pltpu.VMEM((rows, cols), F32),
        ),
        in_specs=[FAR] * 3,
        out_specs=(WHOLE,) * 3,
        scratch_shapes=[
            pltpu.VMEM((rows, cols), BF16),
            pltpu.VMEM((rows, cols), BF16),
            pltpu.VMEM((rank, cols), F32),
            pltpu.SemaphoreType.DMA((3, len(parts))),
        ],
        compiler_params=params(58),
        name="left_term",
    )(grad[0], error[0], q_start.T)
    one, three, two = (
        lax.ppermute(term, "dp", [(i, (i + k) % groups) for i in range(groups)]) for k in (1, 3, 2)
    )
    given, gram, left = pl.pallas_call(
        given_kernel,
        out_shape=(
            pltpu.VMEM((rank, half + LANES), F32),
            pltpu.VMEM((TILE, LANES), F32),
            pltpu.VMEM((rank, rows), F32),
        ),
        in_specs=[WHOLE] * 5,
        out_specs=(WHOLE,) * 3,
        compiler_params=params(8),
        name="right_given",
    )(term, one, three, two, merged)
    taken = lax.ppermute(given, "core", swap)
    kept = pl.pallas_call(
        kept_kernel,
        out_shape=pltpu.VMEM((rank, half), F32),
        in_specs=[WHOLE] * 2,
        out_specs=WHOLE,
        compiler_params=params(8),
        cost_estimate=cost(2 * rank * rows * half, 4 * rows * half),
        name="right_kept",
    )(left, merged)
    pieces = pl.pallas_call(
        pieces_kernel,
        out_shape=pltpu.VMEM((planes, tiles + 1, TILE, LANES), F32),
        in_specs=[WHOLE] * 3,
        out_specs=WHOLE,
        compiler_params=params(8),
        name="right_pieces",
    )(kept, gram, taken)
    arrived = lax.all_to_all(pieces, ("dp", "x"), 0, 0)
    spread = pl.pallas_call(
        plane_kernel,
        out_shape=pltpu.VMEM((layers, tiles + 1, TILE, LANES), F32),
        in_specs=[WHOLE],
        out_specs=WHOLE,
        compiler_params=params(8),
        name="plane_sum",
    )(arrived)
    arrived = lax.all_to_all(spread, "z", 0, 0)
    spread, gram = pl.pallas_call(
        functools.partial(layer_kernel, groups),
        out_shape=(pltpu.VMEM((planes, tiles, TILE, LANES), F32), pltpu.VMEM((TILE, LANES), F32)),
        in_specs=[WHOLE],
        out_specs=(WHOLE,) * 2,
        compiler_params=params(8),
        name="layer_sum",
    )(arrived)
    own = lax.all_to_all(spread, ("dp", "x"), 0, 0)
    chunks = 4
    shapes = (((rows, cols), BF16), ((rows, cols), F32), ((rank, cols), F32))
    out_shapes = tuple(jax.ShapeDtypeStruct(shape, dtype) for shape, dtype in shapes)
    factor_shape = pltpu.VMEM((rows + rank, 6 * rank), BF16)

    def scratch(halves):
        buffers = [pltpu.VMEM((shape[0], halves * half), dtype) for shape, dtype in shapes]
        return buffers + [pltpu.SemaphoreType.DMA((3, halves * chunks))]

    ahead, *begun = pl.pallas_call(
        functools.partial(ahead_kernel, groups, chunks),
        out_shape=(factor_shape,) + out_shapes,
        in_specs=[WHOLE] * 5,
        out_specs=(WHOLE,) + (FAR,) * 3,
        scratch_shapes=scratch(1),
        compiler_params=params(8),
        name="outputs_ahead",
    )(gram, left, own, base, momentum)
    own, ahead = lax.optimization_barrier((own, ahead))
    other = lax.ppermute(own, "core", swap)
    beside = pl.pallas_call(
        functools.partial(factor_kernel, groups),
        out_shape=factor_shape,
        in_specs=[WHOLE] * 2,
        out_specs=WHOLE,
        compiler_params=params(8),
        cost_estimate=cost(8 * rank * rows * LANES, 4 * rows * LANES),
        name="factors",
    )(gram, left)
    new_error, new_momentum, q_next = pl.pallas_call(
        functools.partial(output_kernel, chunks),
        out_shape=out_shapes,
        in_specs=[WHOLE] * 6 + [FAR] * 3,
        out_specs=(FAR,) * 3,
        scratch_shapes=scratch(2),
        input_output_aliases={6: 0, 7: 1, 8: 2},
        compiler_params=params(12),
        name="outputs",
    )(ahead, beside, own, other, base, momentum, *begun)
    return (new_error[None], new_momentum, q_next.T)


def solution(mesh):
    shape = mesh.shape
    fine = Mesh(mesh.devices.reshape(shape["dp"], 4, 8, 2), ("dp", "x", "z", "core"))
    rows = ("x", "z", "core")
    placed = (P("dp", rows, None), P("dp", rows, None), P(rows, None), P())
    return jax.shard_map(
        shards,
        mesh=fine,
        in_specs=placed,
        out_specs=(P("dp", rows, None), P(rows, None), P()),
        check_vma=False,
    )
```

```python
import functools
import jax
import jax.numpy as jnp
from jax import lax
from jax.experimental import pallas as pl
from jax.experimental.pallas import tpu as pltpu
from jax.sharding import Mesh, PartitionSpec as P

HIGHEST = lax.Precision.HIGHEST
F32 = jnp.float32
BF16 = jnp.bfloat16
LANES = 128
TILE = 8
WHOLE = pl.BlockSpec(memory_space=pltpu.VMEM)
FAR = pl.BlockSpec(memory_space=pltpu.HBM)


def split3(value):
    high = value.astype(BF16)
    rest = value - high.astype(F32)
    middle = rest.astype(BF16)
    low = (rest - middle.astype(F32)).astype(BF16)
    return high, middle, low


def nt_dot(first, second, precision=None):
    return lax.dot_general(
        first, second, (((1,), (1,)), ((), ())), precision=precision, preferred_element_type=F32
    )


def left_kernel(parts, grad, error, q_start, term, merged, base, grad_vmem, error_vmem, q_vmem, sems):
    unit = grad.shape[1] // sum(parts)
    slabs = [pl.ds(sum(parts[:step]) * unit, parts[step] * unit) for step in range(len(parts))]
    copies = []
    for step, here in enumerate(slabs):
        group = [
            pltpu.make_async_copy(far.at[:, here], near.at[:, here], sems.at[which, step])
            for which, (far, near) in enumerate(
                ((grad, grad_vmem), (error, error_vmem), (q_start, q_vmem))
            )
        ]
        for copy in group:
            copy.start()
        copies.append(group)
    total = jnp.zeros(term.shape, F32)
    for group, here in zip(copies, slabs):
        for copy in group:
            copy.wait()
        summed = grad_vmem[:, here].astype(F32) + error_vmem[:, here].astype(F32)
        base[:, here] = summed
        low = summed.astype(BF16)
        merged[:, here] = low
        total += nt_dot(q_vmem[:, here].astype(BF16), low)
    term[...] = total


def given_kernel(term, one, three, two, merged, given, gram, left):
    half = merged.shape[1] // 2
    rank = term.shape[0]
    total = (term[...] + two[...]) + (one[...] + three[...])
    left[...] = total
    there = pl.ds(pl.multiple_of((1 - lax.axis_index("core")) * half, LANES), half)
    given[:, :half] = jnp.dot(total.astype(BF16), merged[:, there], preferred_element_type=F32)
    square = nt_dot(total, total, HIGHEST)
    rest = jnp.zeros((TILE, LANES - 2 * rank), F32)
    tile = jnp.concatenate([square[:TILE], square[TILE:], rest], axis=1)
    gram[...] = tile
    given[:TILE, half:] = tile
    given[TILE:, half:] = jnp.zeros((rank - TILE, LANES), F32)


def kept_kernel(left, merged, kept):
    half = merged.shape[1] // 2
    here = pl.ds(pl.multiple_of(lax.axis_index("core") * half, LANES), half)
    kept[...] = jnp.dot(left[...].astype(BF16), merged[:, here], preferred_element_type=F32)


def pieces_kernel(kept, gram, taken, pieces):
    half = kept.shape[1]
    planes, tiles = pieces.shape[:2]
    across = (tiles - 1) // 2
    square = gram[...] + taken[:TILE, half:]
    for index in range(planes):
        for block in range(across):
            here = pl.ds((index * across + block) * LANES, LANES)
            total = kept[:, here] + taken[:, here]
            pieces[index, block] = total[:TILE]
            pieces[index, across + block] = total[TILE:]
        pieces[index, tiles - 1] = square


def plane_kernel(arrived, spread):
    total = arrived[0]
    for index in range(1, arrived.shape[0]):
        total += arrived[index]
    for index in range(spread.shape[0]):
        spread[index] = total


def layer_kernel(groups, arrived, spread, gram):
    tiles = spread.shape[1]
    total = arrived[0]
    for index in range(1, arrived.shape[0]):
        total += arrived[index]
    gram[...] = total[tiles] / groups
    for index in range(spread.shape[0]):
        spread[index] = total[:tiles]


def make_factors(groups, gram, left, factors):
    rank, rows = left.shape
    shape = (rank, LANES)
    row = lax.broadcasted_iota(jnp.int32, shape, 0)
    col = lax.broadcasted_iota(jnp.int32, shape, 1)
    third = (col >= rank) & (col < 2 * rank)
    square = jnp.concatenate([gram[:, :rank], gram[:, rank : 2 * rank]], axis=0)
    rest = jnp.zeros((rank, LANES - 2 * rank - rows), F32)
    table = jnp.concatenate([square, jnp.zeros((rank, rank), F32), left[...], rest], axis=1)
    table = jnp.where(col == row + rank, 1.0, table)
    pivots = jnp.ones(shape, F32)
    for step in range(rank):
        column = jnp.broadcast_to(table[:, step : step + 1], shape)
        scaled = table[step : step + 1, :] / column[step : step + 1, :]
        pivots = jnp.where(row == step, column, pivots)
        change = jnp.where((row < step) & third, 0.0, column * scaled)
        table = jnp.where(row == step, scaled, table - change)
    table = jnp.where(third, table * jnp.sqrt(pivots), table)
    combined = table[:, 2 * rank : 2 * rank + rows].T
    stacked = jnp.concatenate([combined, table[:, rank : 2 * rank]], axis=0) / groups
    high, middle, low = split3(stacked)
    factors[...] = jnp.concatenate([high, high, middle, high, middle, low], axis=1)


def put_halves(chunks, halves, factors, base, momentum, outs, scratch):
    error_vmem, momentum_vmem, q_vmem, sems = scratch
    rows, cols = base.shape
    half = cols // 2
    width = half // chunks
    copies = []
    for turn, (begin, source) in enumerate(halves):
        across = source.shape[1] // 2
        per = width // (across * LANES)
        for chunk in range(chunks):
            parts = []
            for index in range(chunk * per, (chunk + 1) * per):
                for block in range(across):
                    parts.append(jnp.concatenate([source[index, block], source[index, across + block]], axis=0))
            high, middle, low = split3(jnp.concatenate(parts, axis=1))
            depth = jnp.concatenate([high, middle, high, low, middle, high], axis=0)
            product = jnp.dot(factors[...], depth, preferred_element_type=F32)
            approx = product[:rows]
            here = pl.ds(turn * half + chunk * width, width)
            there = pl.ds(begin + chunk * width, width)
            q_vmem[:, here] = product[rows:]
            error_vmem[:, here] = (base[:, there] - approx).astype(BF16)
            momentum_vmem[:, here] = 0.9 * momentum[:, there] + approx
            for which, (near, far) in enumerate(zip((error_vmem, momentum_vmem, q_vmem), outs)):
                copy = pltpu.make_async_copy(
                    near.at[:, here], far.at[:, there], sems.at[which, turn * chunks + chunk]
                )
                copy.start()
                copies.append(copy)
    for copy in copies:
        copy.wait()


def ahead_kernel(groups, chunks, gram, left, own, base, momentum, factors, *rest):
    @pl.when(lax.axis_index("core") == 1)
    def _():
        make_factors(groups, gram, left, factors)
        half = base.shape[1] // 2
        put_halves(chunks, ((half, own),), factors, base, momentum, rest[:3], rest[3:])


def factor_kernel(groups, gram, left, factors):
    @pl.when(lax.axis_index("core") == 0)
    def _():
        make_factors(groups, gram, left, factors)


def output_kernel(chunks, ahead, beside, own, other, base, momentum, *rest):
    outs, scratch = rest[3:6], rest[6:]
    half = base.shape[1] // 2
    core = lax.axis_index("core")

    @pl.when(core == 0)
    def _():
        put_halves(chunks, ((0, own), (half, other)), beside, base, momentum, outs, scratch)

    @pl.when(core == 1)
    def _():
        put_halves(chunks, ((0, other),), ahead, base, momentum, outs, scratch)


def params(megabytes):
    return pltpu.CompilerParams(vmem_limit_bytes=megabytes * 1024 * 1024)


def cost(flops, moved):
    return pl.CostEstimate(flops=flops, bytes_accessed=moved, transcendentals=0)


def exchange(array, axes):
    flat = array.reshape(array.shape[0], -1, LANES)
    return lax.all_to_all(flat, axes, 0, 0).reshape(array.shape)


def shards(grad, error, momentum, q_start):
    groups = lax.axis_size("dp")
    planes = groups * lax.axis_size("x")
    layers = lax.axis_size("z")
    cols, rank = q_start.shape
    rows = grad.shape[1]
    half = cols // 2
    tiles = rank * half // planes // (TILE * LANES)
    swap = [(0, 1), (1, 0)]
    parts = (1,) * 6

    term, merged, base = pl.pallas_call(
        functools.partial(left_kernel, parts),
        out_shape=(
            pltpu.VMEM((rank, rows), F32),
            pltpu.VMEM((rows, cols), BF16),
            pltpu.VMEM((rows, cols), F32),
        ),
        in_specs=[FAR] * 3,
        out_specs=(WHOLE,) * 3,
        scratch_shapes=[
            pltpu.VMEM((rows, cols), BF16),
            pltpu.VMEM((rows, cols), BF16),
            pltpu.VMEM((rank, cols), F32),
            pltpu.SemaphoreType.DMA((3, len(parts))),
        ],
        compiler_params=params(58),
        name="left_term",
    )(grad[0], error[0], q_start.T)
    one, three, two = (
        lax.ppermute(term, "dp", [(i, (i + k) % groups) for i in range(groups)]) for k in (1, 3, 2)
    )
    given, gram, left = pl.pallas_call(
        given_kernel,
        out_shape=(
            pltpu.VMEM((rank, half + LANES), F32),
            pltpu.VMEM((TILE, LANES), F32),
            pltpu.VMEM((rank, rows), F32),
        ),
        in_specs=[WHOLE] * 5,
        out_specs=(WHOLE,) * 3,
        compiler_params=params(8),
        name="right_given",
    )(term, one, three, two, merged)
    taken = lax.ppermute(given, "core", swap)
    kept = pl.pallas_call(
        kept_kernel,
        out_shape=pltpu.VMEM((rank, half), F32),
        in_specs=[WHOLE] * 2,
        out_specs=WHOLE,
        compiler_params=params(8),
        cost_estimate=cost(2 * rank * rows * half, 4 * rows * half),
        name="right_kept",
    )(left, merged)
    pieces = pl.pallas_call(
        pieces_kernel,
        out_shape=pltpu.VMEM((planes, tiles + 1, TILE, LANES), F32),
        in_specs=[WHOLE] * 3,
        out_specs=WHOLE,
        compiler_params=params(8),
        name="right_pieces",
    )(kept, gram, taken)
    arrived = exchange(pieces, ("dp", "x"))
    spread = pl.pallas_call(
        plane_kernel,
        out_shape=pltpu.VMEM((layers, tiles + 1, TILE, LANES), F32),
        in_specs=[WHOLE],
        out_specs=WHOLE,
        compiler_params=params(8),
        name="plane_sum",
    )(arrived)
    arrived = exchange(spread, "z")
    spread, gram = pl.pallas_call(
        functools.partial(layer_kernel, groups),
        out_shape=(pltpu.VMEM((planes, tiles, TILE, LANES), F32), pltpu.VMEM((TILE, LANES), F32)),
        in_specs=[WHOLE],
        out_specs=(WHOLE,) * 2,
        compiler_params=params(8),
        name="layer_sum",
    )(arrived)
    own = exchange(spread, ("dp", "x"))
    chunks = 4
    shapes = (((rows, cols), BF16), ((rows, cols), F32), ((rank, cols), F32))
    out_shapes = tuple(jax.ShapeDtypeStruct(shape, dtype) for shape, dtype in shapes)
    factor_shape = pltpu.VMEM((rows + rank, 6 * rank), BF16)

    def scratch(halves):
        buffers = [pltpu.VMEM((shape[0], halves * half), dtype) for shape, dtype in shapes]
        return buffers + [pltpu.SemaphoreType.DMA((3, halves * chunks))]

    ahead, *begun = pl.pallas_call(
        functools.partial(ahead_kernel, groups, chunks),
        out_shape=(factor_shape,) + out_shapes,
        in_specs=[WHOLE] * 5,
        out_specs=(WHOLE,) + (FAR,) * 3,
        scratch_shapes=scratch(1),
        compiler_params=params(8),
        name="outputs_ahead",
    )(gram, left, own, base, momentum)
    own, ahead = lax.optimization_barrier((own, ahead))
    other = lax.ppermute(own, "core", swap)
    beside = pl.pallas_call(
        functools.partial(factor_kernel, groups),
        out_shape=factor_shape,
        in_specs=[WHOLE] * 2,
        out_specs=WHOLE,
        compiler_params=params(8),
        cost_estimate=cost(8 * rank * rows * LANES, 4 * rows * LANES),
        name="factors",
    )(gram, left)
    new_error, new_momentum, q_next = pl.pallas_call(
        functools.partial(output_kernel, chunks),
        out_shape=out_shapes,
        in_specs=[WHOLE] * 6 + [FAR] * 3,
        out_specs=(FAR,) * 3,
        scratch_shapes=scratch(2),
        input_output_aliases={6: 0, 7: 1, 8: 2},
        compiler_params=params(12),
        name="outputs",
    )(ahead, beside, own, other, base, momentum, *begun)
    return (new_error[None], new_momentum, q_next.T)


def solution(mesh):
    shape = mesh.shape
    fine = Mesh(mesh.devices.reshape(shape["dp"], 4, 8, 2), ("dp", "x", "z", "core"))
    rows = ("x", "z", "core")
    placed = (P("dp", rows, None), P("dp", rows, None), P(rows, None), P())
    return jax.shard_map(
        shards,
        mesh=fine,
        in_specs=placed,
        out_specs=(P("dp", rows, None), P(rows, None), P()),
        check_vma=False,
    )
```
